768 devices in a mesh: dom: 12 (over z), grp: 64 (over y, x, core).
Axes of the slice: x: 4, y: 8, z: 12, core: 2. Of those that a mesh axis runs over, the one named last changes fastest.
Arguments:
- positions: float32 [3, 1572864], P(None, ('dom', 'grp')), may hold values from -6 to 6
- velocities: float32 [3, 1572864], P(None, ('dom', 'grp')), may hold values from -6 to 6
- masses: float32 [1572864], P(('dom', 'grp')), may hold values from 1 to 16
- atom_kinds: int32 [1572864], P(('dom', 'grp')), may hold values from 0 to 99
- frag_atoms: int32 [24576, 64], P(('dom', 'grp')), may hold values from -1 to 2175, as said below
- assign: int32 [2, 24576], P(None, ('dom', 'grp')), may hold values from -1 to 63, as said below
- embed_table: bfloat16 [100, 256], replicated, may hold values from -8 to 8
- neigh_table: bfloat16 [100, 256], replicated, may hold values from -2 to 2
- w_query: bfloat16 [256, 256], replicated, may hold values from -0.375 to 0.375
- w_key: bfloat16 [256, 256], replicated, may hold values from -0.375 to 0.375
- w_value: bfloat16 [256, 256], replicated, may hold values from -0.375 to 0.375
- w_energy: float32 [256], replicated, may hold values from -0.375 to 0.375
- w_force: float32 [256, 8], replicated, may hold values from -0.375 to 0.375
- head_decay: float32 [8], replicated, may hold values from 0.05 to 1
Outputs:
- positions_out: float32 [3, 1572864], P(None, ('dom', 'grp'))
- velocities_out: float32 [3, 1572864], P(None, ('dom', 'grp'))
- energies: float32 [2, 24576], P(None, ('dom', 'grp'))
The draws below stay inside these ranges and needn't reach their ends.
Inputs may be any that keep to these rules, and one draw needn't show every extreme that they name: `frag_atoms`: entries -1 mark padding; a slot's live indices come first and run consecutively. Slots that are not active in a step have no live indices. `assign`: the active slots are the same in every step. Among the slots of one device, at most 2 name the same grp index in a step, and among the devices of one dom index at most 16 slots name the same grp index in a step.
All inputs are finite; a program needn't handle non-finite values.
Results may differ from the reference program's by a relative error of at most 0.0076.
Values sent between devices are 32-bit elements; how exact they have to be, the bound alone decides.
A program may use at most 32 MiB of HBM per device.

```python
import math
import jax
import jax.numpy as jnp
from jax import lax

HID = 256
HEADS = 8
TYPES = 100
ATOMS = 64
HALO = 64
STEPS = 2
ATOM_DEV = 2048
RECV = 16
FRAG_MAX = 32
CAP = 2
ATOM_EXT = 2176
ATOMS_ALL = 1572864
N_DOM = 12
N_GRP = 64


def domain_layout(key):
    key = jax.random.fold_in(key, 11)
    dev_total = N_DOM * N_GRP
    dev_keys = jax.random.split(key, dev_total)
    orders = jax.vmap(lambda one_key: jax.random.permutation(one_key, FRAG_MAX))(dev_keys).astype(jnp.int32)
    rank_key = jax.random.fold_in(key, 5)
    rank_owner = jax.vmap(lambda one_key: jax.random.permutation(one_key, N_GRP))(jax.random.split(rank_key, N_DOM)).astype(jnp.int32)
    return (orders, rank_owner)


def rank_loads():
    pair_total = RECV // CAP
    busy_ranks = N_GRP // 4
    heaviest = FRAG_MAX // CAP
    remainder = N_GRP * pair_total - busy_ranks * heaviest
    light_ranks = N_GRP - busy_ranks
    rank_ids = jnp.arange(N_GRP, dtype=jnp.int32)
    extra = (rank_ids - busy_ranks < remainder % light_ranks).astype(jnp.int32)
    return jnp.where(rank_ids < busy_ranks, heaviest, remainder // light_ranks + extra).astype(jnp.int32)


def draw_assign(key, part):
    orders, rank_owner = domain_layout(key)
    key = jax.random.fold_in(key, 23)
    loads_now = rank_loads()
    first_pick = jnp.cumsum(loads_now) - loads_now
    pair_total = RECV // CAP
    pick_ids = jnp.arange(N_GRP * pair_total, dtype=jnp.int32)
    pick_rank = jnp.sum((first_pick[None, :] <= pick_ids[:, None]).astype(jnp.int32), axis=1) - 1
    within = pick_ids - first_pick[pick_rank]
    lane = jnp.arange(CAP, dtype=jnp.int32)
    outputs = []
    for md_step in range(STEPS):
        step_key = jax.random.fold_in(key, md_step)
        receivers = jax.vmap(lambda one_key: jax.random.permutation(one_key, N_GRP))(jax.random.split(step_key, N_DOM)).astype(jnp.int32)
        sender = rank_owner[:, pick_rank]
        target = receivers[:, pick_ids % N_GRP]
        device = jnp.arange(N_DOM, dtype=jnp.int32)[:, None] * N_GRP + sender
        position = CAP * within[None, :, None] + lane[None, None, :]
        slot_ids = orders[device[:, :, None], position]
        flat_slot = (device[:, :, None] * FRAG_MAX + slot_ids).reshape(-1)
        target_all = jnp.broadcast_to(target[:, :, None], slot_ids.shape).reshape(-1)
        receiver_of = jnp.full((N_DOM * N_GRP * FRAG_MAX,), -1, jnp.int32).at[flat_slot].set(target_all)
        outputs.append(receiver_of)
    return jnp.stack(outputs).astype(jnp.int32)


def draw_frag_atoms(key, part):
    orders, rank_owner = domain_layout(key)
    key = jax.random.fold_in(key, 37)
    dev_total = N_DOM * N_GRP
    loads_now = rank_loads()
    dom_rows = jnp.arange(N_DOM, dtype=jnp.int32)[:, None]
    device_rank = jnp.zeros((N_DOM, N_GRP), jnp.int32).at[dom_rows, rank_owner].set(jnp.broadcast_to(jnp.arange(N_GRP, dtype=jnp.int32)[None, :], (N_DOM, N_GRP)))
    device_load = loads_now[device_rank].reshape(dev_total)
    place_of = jnp.argsort(orders, axis=1).astype(jnp.int32)
    occupied = place_of < (CAP * device_load)[:, None]
    count_key, start_key = jax.random.split(key)
    atom_totals = jax.random.randint(count_key, (dev_total, FRAG_MAX), ATOMS // 3, ATOMS + 1).astype(jnp.int32)
    atom_totals = jnp.where(place_of == 0, ATOMS, atom_totals)
    start_room = ATOM_EXT - atom_totals + 1
    first_atom = jax.random.randint(start_key, (dev_total, FRAG_MAX), 0, 1048576).astype(jnp.int32) % start_room
    first_atom = jnp.where(place_of == 0, ATOM_EXT - ATOMS, first_atom)
    offsets = jnp.arange(ATOMS, dtype=jnp.int32)
    indices = first_atom[:, :, None] + offsets[None, None, :]
    present = (offsets[None, None, :] < atom_totals[:, :, None]) & occupied[:, :, None]
    return jnp.where(present, indices, -1).reshape(dev_total * FRAG_MAX, ATOMS).astype(jnp.int32)


def set_ends(result, stream_key, least, top_value):
    longest = result.shape.index(max(result.shape))
    spots = []
    for shift in (0, 1):
        where = [jax.random.randint(jax.random.fold_in(stream_key, axis), (), 0, length) for axis, length in enumerate(result.shape)]
        where[longest] = (where[longest] + shift) % result.shape[longest]
        spots.append(tuple(where))
    return result.at[spots[0]].set(least).at[spots[1]].set(top_value)


def block_scale(key, shape, shards, least, largest):
    loudness, own = 1.0, jax.random.fold_in(key, 6)
    for dim, blocks in shards:
        draws = jnp.exp(jax.random.uniform(jax.random.fold_in(own, dim), (blocks,), jnp.float32, least / len(shards), largest / len(shards)))
        loudness = loudness * jnp.repeat(draws, shape[dim] // blocks).reshape([-1 if axis == dim else 1 for axis in range(len(shape))])
    return loudness


def gaussian(stream_key, shape, scale, limit, cuts=(), kind=jnp.bfloat16):
    array = jax.random.normal(stream_key, shape, jnp.float32) * scale
    if len(cuts) > 0:
        array = block_scale(stream_key, shape, cuts, -0.22, 0.18) * array
    return jnp.clip(array, min=-limit, max=limit).astype(kind)


def setup_inputs(seed: int = 0) -> dict:
    streams_of = jax.random.split(jax.random.key(seed), 15)
    positions = gaussian(streams_of[0], (3, ATOMS_ALL), 1.0, 6.0, ((1, 768),), jnp.float32)
    velocities = gaussian(streams_of[1], (3, ATOMS_ALL), 1.0, 6.0, ((1, 768),), jnp.float32)
    masses = jnp.clip(jnp.exp(math.log(16.0) - 2.7725887 * jax.random.uniform(streams_of[2], (ATOMS_ALL,), jnp.float32) ** block_scale(streams_of[2], (ATOMS_ALL,), ((0, 768),), -0.2, 0.2)), 1.0, 16.0)
    atom_kinds = set_ends(jax.random.randint(streams_of[3], (ATOMS_ALL,), 0, TYPES), jax.random.fold_in(streams_of[3], 1), 0, TYPES - 1).astype(jnp.int32)
    frag_atoms = draw_frag_atoms(jax.random.fold_in(streams_of[14], 71), 0)
    assign = draw_assign(jax.random.fold_in(streams_of[14], 71), 0)
    embed_table = gaussian(streams_of[6], (TYPES, HID), 1.5, 8.0)
    neigh_table = gaussian(streams_of[7], (TYPES, HID), 0.3, 2.0)
    w_query = gaussian(streams_of[8], (HID, HID), HID ** -0.5, 0.375)
    w_key = gaussian(streams_of[9], (HID, HID), HID ** -0.5, 0.375)
    w_value = gaussian(streams_of[10], (HID, HID), HID ** -0.5, 0.375)
    w_energy = gaussian(streams_of[11], (HID,), HID ** -0.5, 0.375, (), jnp.float32)
    w_force = gaussian(streams_of[12], (HID, HEADS), HID ** -0.5, 0.375, (), jnp.float32)
    head_decay = jnp.clip(jnp.exp(jax.random.uniform(streams_of[13], (HEADS,), jnp.float32, math.log(0.05), math.log(1.0))), 0.05, 1.0)
    return dict(positions=positions, velocities=velocities, masses=masses, atom_kinds=atom_kinds, frag_atoms=frag_atoms, assign=assign, embed_table=embed_table, neigh_table=neigh_table, w_query=w_query, w_key=w_key, w_value=w_value, w_energy=w_energy, w_force=w_force, head_decay=head_decay)


TIME_STEP = 0.05
NEAR_RATE = 0.5
HIGHEST_MODE = lax.Precision.HIGHEST

def fragment_model(coords, kinds, embed_table, neigh_table, w_query, w_key, w_value, w_energy, w_force, head_decay):
    frag_count, atom_count = kinds.shape
    model_width = w_query.shape[0]
    head_count = head_decay.shape[0]
    head_width = model_width // head_count
    atom_mask = (kinds >= 0).astype(jnp.float32)
    pair_mask = atom_mask[:, :, None] * atom_mask[:, None, :]
    squared = jnp.zeros((frag_count, atom_count, atom_count), jnp.float32)
    for component in range(3):
        column = coords[:, component, :]
        spread = column[:, :, None] - column[:, None, :]
        squared = squared + spread * spread
    kind_ids = jnp.arange(embed_table.shape[0]).astype(jnp.float32)
    one_hot = (kinds[:, :, None] == kind_ids[None, None, :]).astype(jnp.float32)
    others = 1.0 - jnp.eye(atom_count, dtype=jnp.float32)
    nearby = jnp.exp(-NEAR_RATE * squared) * pair_mask * others[None]
    tallies = jnp.einsum('fij,fjt->fit', nearby, one_hot, precision=HIGHEST_MODE)
    summed = jnp.einsum('fit,tc->fic', one_hot, embed_table.astype(jnp.float32), precision=HIGHEST_MODE)
    summed = summed + jnp.einsum('fit,tc->fic', tallies, neigh_table.astype(jnp.float32), precision=HIGHEST_MODE)
    hidden = (jax.nn.silu(summed) * atom_mask[:, :, None]).astype(jnp.bfloat16)
    row_block = hidden.reshape(frag_count * atom_count, model_width)
    split_shape = (frag_count, atom_count, head_count, head_width)
    query_rows = jnp.dot(row_block, w_query, preferred_element_type=jnp.float32).astype(jnp.bfloat16).reshape(split_shape)
    key_rows = jnp.dot(row_block, w_key, preferred_element_type=jnp.float32).astype(jnp.bfloat16).reshape(split_shape)
    value_rows = jnp.dot(row_block, w_value, preferred_element_type=jnp.float32).astype(jnp.bfloat16).reshape(split_shape)
    scores = jnp.einsum('fihd,fjhd->fhij', query_rows.astype(jnp.float32), key_rows.astype(jnp.float32)) / math.sqrt(head_width)
    envelope = jnp.exp(-head_decay[None, :, None, None] * squared[:, None, :, :])
    weights = jax.nn.silu(scores) * envelope * pair_mask[:, None, :, :]
    rounded = weights.astype(jnp.bfloat16)
    mixture = jnp.einsum('fhij,fjhd->fihd', rounded.astype(jnp.float32), value_rows.astype(jnp.float32))
    updated = hidden.astype(jnp.float32) + mixture.reshape(frag_count, atom_count, model_width)
    flat_state = updated.reshape(frag_count * atom_count, model_width)
    atom_energy = jnp.dot(flat_state, w_energy, precision=HIGHEST_MODE).reshape(frag_count, atom_count) * atom_mask
    scalars = jnp.dot(flat_state, w_force, precision=HIGHEST_MODE).reshape(frag_count, atom_count, head_count)
    coupling = jnp.einsum('fhij,fjh->fij', weights, scalars, precision=HIGHEST_MODE)
    row_total = lax.optimization_barrier(jnp.sum(coupling, axis=2))
    pulled = jnp.einsum('fij,fcj->fci', coupling, coords, precision=HIGHEST_MODE)
    forces = (coords * row_total[:, None, :] - pulled) * atom_mask[:, None, :]
    return (forces, atom_energy)

def reference(positions, velocities, masses, atom_kinds, frag_atoms, assign, embed_table, neigh_table, w_query, w_key, w_value, w_energy, w_force, head_decay):
    dev_total = N_DOM * N_GRP
    ext_width = ATOM_DEV + 2 * HALO
    index_rows = frag_atoms.reshape(dev_total, FRAG_MAX * ATOMS)
    real_atom = index_rows >= 0
    safe_index = jnp.maximum(index_rows, 0).astype(jnp.int32)
    dev_offset = (jnp.arange(dev_total, dtype=jnp.int32) * ext_width)[:, None]
    seg_ids = jnp.where(real_atom, safe_index + dev_offset, dev_total * ext_width).reshape(-1).astype(jnp.int32)

    def extend(field):
        channels = field.shape[0]
        blocks = field.reshape(channels, N_DOM, N_GRP, ATOM_DEV)
        lower_rim = jnp.roll(blocks, 1, axis=1)[..., ATOM_DEV - HALO:]
        upper_rim = jnp.roll(blocks, -1, axis=1)[..., :HALO]
        return jnp.concatenate([lower_rim, blocks, upper_rim], axis=3).reshape(channels, dev_total, ext_width)

    def select(extended):
        return jnp.take_along_axis(extended, jnp.broadcast_to(safe_index[None], (extended.shape[0],) + safe_index.shape), axis=2)
    kinds_float = atom_kinds.astype(jnp.float32)[None, :]
    kinds_base = jnp.where(real_atom, select(extend(kinds_float))[0], -1.0)

    def one_device(pieces):
        return fragment_model(pieces[0], pieces[1], embed_table, neigh_table, w_query, w_key, w_value, w_energy, w_force, head_decay)
    energies = []
    for md_step in range(STEPS):
        active = assign[md_step].reshape(dev_total, FRAG_MAX) >= 0
        frag_kinds = jnp.where(jnp.repeat(active, ATOMS, axis=1), kinds_base, -1.0)
        frag_pos = select(extend(positions))
        coords = frag_pos.reshape(3, dev_total, FRAG_MAX, ATOMS).transpose(1, 2, 0, 3)
        kinds_rows = frag_kinds.reshape(dev_total, FRAG_MAX, ATOMS)
        forces, atom_energy = lax.map(one_device, (coords, kinds_rows))
        energies.append(lax.optimization_barrier(jnp.sum(atom_energy, axis=2)).reshape(-1))
        force_rows = forces.transpose(2, 0, 1, 3).reshape(3, -1)
        gathered = jax.ops.segment_sum(force_rows.T, seg_ids, num_segments=dev_total * ext_width + 1)[:-1]
        force_ext = gathered.T.reshape(3, N_DOM, N_GRP, ext_width)
        middle = force_ext[..., HALO:HALO + ATOM_DEV]
        from_upper = jnp.roll(force_ext[..., :HALO], -1, axis=1)
        from_lower = jnp.roll(force_ext[..., HALO + ATOM_DEV:], 1, axis=1)
        summed_force = middle.at[..., :HALO].add(from_lower).at[..., ATOM_DEV - HALO:].add(from_upper)
        summed_force = summed_force.reshape(3, dev_total * ATOM_DEV)
        velocities = velocities + TIME_STEP * summed_force / masses[None, :]
        positions = positions + TIME_STEP * velocities
    return (positions, velocities, jnp.stack(energies))
```

```python
import functools
import math

import jax
import jax.numpy as jnp
from jax import lax
from jax.experimental import pallas as pl
from jax.experimental.pallas import tpu as pltpu
from jax.sharding import PartitionSpec as P

HALO = 64
STEPS = 2
TIME_STEP = 0.05
NEAR_RATE = 0.5
FAR = 1e30
LANES = 128
GROUP = 4
F32 = jnp.float32
BF16 = jnp.bfloat16
HIGHEST = lax.Precision.HIGHEST


def dot_nn(a, b, precision=None):
    return lax.dot_general(
        a, b, (((1,), (0,)), ((), ())), precision=precision, preferred_element_type=F32
    )


def dot_nt(a, b):
    return lax.dot_general(a, b, (((1,), (1,)), ((), ())), preferred_element_type=F32)


def lane_pick(x, index):
    return jnp.take_along_axis(x, index, axis=1, mode="promise_in_bounds")


def iota(shape, dim):
    return lax.broadcasted_iota(jnp.int32, shape, dim)


def to_row(column):
    size = column.shape[0]
    same = iota((size, size), 0) == iota((size, size), 1)
    return jnp.sum(jnp.where(same, column, 0.0), axis=0, keepdims=True)


def to_column(row):
    size = row.shape[1]
    same = iota((size, size), 0) == iota((size, size), 1)
    return jnp.sum(jnp.where(same, row, 0.0), axis=1, keepdims=True)


def silu_of_double(half):
    return half + half * jnp.tanh(half)


def kernel(
    tiles,
    slots,
    heads,
    positions,
    velocities,
    masses,
    kinds,
    frag_atoms,
    assign,
    embed,
    neigh,
    w_query,
    w_key,
    w_value,
    w_energy,
    w_force,
    head_decay,
    positions_out,
    velocities_out,
    energies_out,
    ext,
    rim_out,
    rim_in,
    table,
    force_pad,
    rows,
    cols,
    counts,
    type_rows,
    pulls,
    atom_energy,
    send_sem,
    recv_sem,
):
    doms = lax.axis_size("dom")
    me = lax.axis_index("dom")
    upper, lower = lax.rem(me + 1, doms), lax.rem(me + doms - 1, doms)
    width = w_query.shape[0]
    head_width = width // heads
    ext_rows = ext.shape[1]
    types = embed.shape[0]

    barrier = pltpu.get_barrier_semaphore()
    for neighbour in (lower, upper):
        pl.semaphore_signal(
            barrier, inc=1, device_id={"dom": neighbour}, device_id_type=pl.DeviceIdType.MESH
        )

    lane = iota((slots, LANES), 1)

    for tile in range(tiles):
        span = pl.ds(tile * LANES, LANES)
        for c in range(3):
            ext[c, tile + 1 : tile + 2, :] = positions[c : c + 1, span]
            ext[4 + c, tile + 1 : tile + 2, :] = velocities[c : c + 1, span]
    ext[3, 1 : tiles + 1, :] = kinds[...].astype(F32)
    ext[7, 1 : tiles + 1, :] = masses[...]
    for c in range(8):
        ext[c, tiles + 2 : ext_rows, :] = jnp.full((ext_rows - tiles - 2, LANES), 1.0, F32)
    for side, row in ((0, tiles), (1, 1)):
        for c in range(8):
            rim_out[0, side, c : c + 1, :] = ext[c, row : row + 1, :]

    def exchange(phase):
        copies = []
        for side, target in ((0, upper), (1, lower)):
            copy = pltpu.make_async_remote_copy(
                src_ref=rim_out.at[phase, side],
                dst_ref=rim_in.at[phase, side],
                send_sem=send_sem.at[phase, side],
                recv_sem=recv_sem.at[phase, side],
                device_id={"dom": target},
                device_id_type=pl.DeviceIdType.MESH,
            )
            copy.start()
            copies.append(copy)
        return copies

    pl.semaphore_wait(barrier, 2)
    copies = exchange(0)

    table[...] = jnp.zeros(table.shape, F32)
    table[0:types, 0:width] = embed[...].astype(F32)
    table[0:types, width : 2 * width] = neigh[...].astype(F32)
    force_pad[...] = jnp.zeros(force_pad.shape, F32)
    force_pad[:, 0:heads] = w_force[...]
    readout = jnp.concatenate(
        [
            jnp.transpose(force_pad[...])[0:heads],
            w_energy[...],
            jnp.zeros((15 - heads, width), F32),
        ],
        axis=0,
    )
    readout_hi = readout.astype(BF16)
    readout = jnp.concatenate(
        [readout_hi, (readout - readout_hi.astype(F32)).astype(BF16)], axis=0
    )

    index = frag_atoms[...]
    live = jnp.where(index >= 0, 1.0, 0.0)
    active = to_column(jnp.where(assign[0:1, :] >= 0, 1.0, 0.0))
    count = jnp.sum(live, axis=1, keepdims=True) * active
    counts[...] = jnp.broadcast_to(count, (slots, LANES))
    start = jnp.maximum(index[:, 0:1], 0) + HALO
    tile_of = lax.shift_right_logical(start, 7)
    shift = jnp.bitwise_and(start, 127)
    both = jnp.concatenate([tile_of, tile_of + 1], axis=0)
    pick = jnp.where(iota((2 * slots, ext_rows), 1) == both, 1.0, 0.0)
    put = jnp.where(
        iota((ext_rows, 2 * slots), 0).astype(F32) == to_row(both.astype(F32)), 1.0, 0.0
    )
    atoms = frag_atoms.shape[1]
    half_lane = jnp.bitwise_and(lane, atoms - 1)
    ahead = half_lane + shift
    pick_lane = jnp.bitwise_and(ahead, 127)
    pick_first = ahead < LANES
    put_lane = jnp.bitwise_and(lane - shift, 127)
    put_first = lane >= shift

    sub8 = iota((8, LANES), 0)
    lane8 = iota((8, LANES), 1)
    lane64 = iota((atoms, LANES), 1)
    sub64 = iota((atoms, LANES), 0)
    left64 = lane64 < atoms
    other = jnp.bitwise_and(lane64, atoms - 1)
    latest = jnp.maximum(sub64, other).astype(F32)
    distinct = sub64 != other
    per_group = LANES // head_width
    groups = heads // per_group
    head_masks = [
        jnp.where(lax.shift_right_logical(lane64, 5) == h, 1.0, 0.0).astype(BF16)
        for h in range(per_group)
    ]
    decay_rows = [
        jnp.where(lane8 < atoms, -head_decay[2 * t], -head_decay[2 * t + 1])[0:1]
        for t in range(heads // 2)
    ]
    flat_masks = [
        jnp.where(sub8 == 2 * t + jnp.where(lane8 < atoms, 0, 1), 1.0, 0.0)
        for t in range(heads // 2)
    ]
    quarter = jnp.bitwise_and(sub8, 3)

    for copy in copies:
        copy.wait()
    for side, row in ((0, 0), (1, tiles + 1)):
        for c in range(8):
            ext[c, row : row + 1, :] = rim_in[0, side, c : c + 1, :]

    def gather(components):
        field = jnp.concatenate([ext[c] for c in components], axis=1)
        picked = dot_nn(pick, field, HIGHEST)
        result = []
        for c in range(len(components)):
            span = slice(c * LANES, (c + 1) * LANES)
            result.append(
                jnp.where(
                    pick_first,
                    lane_pick(picked[0:slots, span], pick_lane),
                    lane_pick(picked[slots:, span], pick_lane),
                )
            )
        return result

    def column(k):
        return lane_pick(cols[...], jnp.full((atoms, LANES), k, jnp.int32))

    def model(group, carry):
        many = range(GROUP)
        slot = [group * GROUP + k for k in many]
        base = pl.multiple_of(group * (GROUP * atoms), GROUP * atoms)
        xyz = [[rows[c, pl.ds(slot[k], 1), :] for c in range(3)] for k in many]
        far = []
        hidden = []
        for k in many:
            squared = None
            for c in range(3):
                spread = column(c * slots + slot[k]) - xyz[k][c]
                squared = spread * spread if squared is None else squared + spread * spread
            far.append(jnp.where(latest < counts[pl.ds(slot[k], 1), :], squared, FAR))
        for k in many:
            nearby = jnp.where(distinct, jnp.exp(-NEAR_RATE * far[k]), 0.0)
            near_hi = nearby.astype(BF16).astype(F32)
            near = jnp.where(left64, near_hi, nearby - near_hi).astype(BF16)
            span = pl.ds(base + k * atoms, atoms)
            theirs = type_rows[span, width : 2 * width]
            summed = dot_nn(near, jnp.concatenate([theirs, theirs], axis=0))
            summed = summed + type_rows[span, 0:width].astype(F32)
            hidden.append(silu_of_double(0.5 * summed).astype(BF16))
        block = jnp.concatenate(hidden, axis=0)
        query = dot_nn(block, w_query[...]).astype(BF16)
        key = dot_nn(block, w_key[...]).astype(BF16)
        value = dot_nn(block, w_value[...]).astype(BF16)
        weights = []
        for k in many:
            mine = slice(k * atoms, (k + 1) * atoms)
            parts = []
            for g in range(groups):
                span = slice(g * LANES, (g + 1) * LANES)
                keys = key[mine, span]
                spread_keys = jnp.concatenate([keys * mask for mask in head_masks], axis=0)
                parts.append(dot_nt(query[mine, span], spread_keys))
            tiles_out = []
            for t in range(heads // 2):
                part = parts[t // 2][:, (t % 2) * LANES : (t % 2 + 1) * LANES]
                half = part * (0.5 / math.sqrt(head_width))
                envelope = jnp.exp(far[k] * decay_rows[t])
                tiles_out.append((silu_of_double(half) * envelope).astype(BF16))
            weights.append(tiles_out)
        for k in many:
            mine = slice(k * atoms, (k + 1) * atoms)
            mixed = []
            for g in range(groups):
                span = slice(g * LANES, (g + 1) * LANES)
                values = value[mine, span]
                spread_values = jnp.concatenate([values * mask for mask in head_masks], axis=0)
                pair = jnp.concatenate(weights[k][2 * g : 2 * g + 2], axis=1)
                mixed.append(dot_nn(pair, spread_values))
            updated = hidden[k].astype(F32) + jnp.concatenate(mixed, axis=1)
            updated_hi = updated.astype(BF16)
            updated_lo = (updated - updated_hi.astype(F32)).astype(BF16)
            scalars = dot_nt(readout, jnp.concatenate([updated_hi, updated_lo], axis=0))
            scalars = scalars[0:16] + scalars[16:32]
            scalars = scalars + pltpu.roll(scalars, atoms, 1)
            atom_energy[pl.ds(slot[k], 1), :] = scalars[heads : heads + 1]
            spots = jnp.where(
                quarter == 0,
                1.0,
                jnp.where(
                    quarter == 1, xyz[k][0], jnp.where(quarter == 2, xyz[k][1], xyz[k][2])
                ),
            )
            left = []
            for t in range(heads // 2):
                flat = jnp.sum(scalars[0:heads] * flat_masks[t], axis=0, keepdims=True)
                term = flat * spots
                term_hi = term.astype(BF16).astype(F32)
                left.append(jnp.where(sub8 < 4, term_hi, term - term_hi))
            left = jnp.concatenate(left, axis=1)
            left = jnp.concatenate([left, jnp.zeros(left.shape, F32)], axis=0).astype(BF16)
            pulled = dot_nt(left, jnp.concatenate(weights[k], axis=1))
            pulls[slot[k], :, 0:atoms] = pulled[0:8]
        return carry

    for step in range(STEPS):
        fields = gather((0, 1, 2, 3) if step == 0 else (0, 1, 2))
        centred = [field - field[:, 0:1] for field in fields[:3]]
        for c in range(3):
            rows[c] = centred[c]
        if step == 0:
            sort = jnp.where(half_lane.astype(F32) < count, fields[3], -1.0)
        else:
            sort = centred[0]
        cols[...] = jnp.transpose(jnp.concatenate(centred + [sort], axis=0))[0:atoms]
        if step == 0:
            both_tables = table[...].astype(BF16)

            def look_up(group, carry):
                base = pl.multiple_of(group * (GROUP * atoms), GROUP * atoms)
                hot = jnp.concatenate(
                    [
                        jnp.where(
                            column(3 * slots + group * GROUP + k) == lane64.astype(F32), 1.0, 0.0
                        )
                        for k in range(GROUP)
                    ],
                    axis=0,
                ).astype(BF16)
                type_rows[pl.ds(base, GROUP * atoms), :] = dot_nn(hot, both_tables).astype(BF16)
                return carry

            lax.fori_loop(0, slots // GROUP, look_up, 0)
        lax.fori_loop(0, slots // GROUP, model, 0)

        energy = jnp.sum(jnp.where(lane < atoms, atom_energy[...], 0.0), axis=1, keepdims=True)
        energies_out[step : step + 1, :] = to_row(energy)
        sums = [pulls[:, q, :] + pulls[:, q + 4, :] for q in range(4)]
        firsts, seconds = [], []
        for c in range(3):
            force = jnp.where(lane < atoms, centred[c] * sums[0] - sums[c + 1], 0.0)
            turned = lane_pick(force, put_lane)
            firsts.append(jnp.where(put_first, turned, 0.0))
            seconds.append(jnp.where(put_first, 0.0, turned))
        placed = jnp.concatenate(
            [jnp.concatenate(firsts, axis=1), jnp.concatenate(seconds, axis=1)], axis=0
        )
        total = dot_nn(put, placed, HIGHEST)
        total = [total[:, c * LANES : (c + 1) * LANES] for c in range(3)]

        phase = step + 1
        for c in range(3):
            rim_out[phase, 0, c : c + 1, :] = total[c][tiles + 1 : tiles + 2]
            rim_out[phase, 0, c + 3 : c + 4, :] = total[c][tiles : tiles + 1]
            rim_out[phase, 1, c : c + 1, :] = total[c][0:1]
            rim_out[phase, 1, c + 3 : c + 4, :] = total[c][1:2]
        for side in range(2):
            rim_out[phase, side, 6:8, :] = jnp.zeros((2, LANES), F32)
        copies = exchange(phase)
        row_id = iota((ext_rows, LANES), 0)
        lane_id = iota((ext_rows, LANES), 1)
        from_lower = lane_id < HALO
        from_upper = lane_id >= LANES - HALO
        for copy in copies:
            copy.wait()
        for c in range(3):
            low = rim_in[phase, 0, c : c + 1, :]
            low_own = rim_in[phase, 0, c + 3 : c + 4, :]
            high = rim_in[phase, 1, c : c + 1, :]
            high_own = rim_in[phase, 1, c + 3 : c + 4, :]
            extra = jnp.where((row_id == 1) & from_lower, low, 0.0)
            extra = jnp.where((row_id == tiles) & from_upper, high, extra)
            extra = jnp.where((row_id == 0) & from_upper, low_own, extra)
            extra = jnp.where((row_id == tiles + 1) & from_lower, high_own, extra)
            moved = ext[4 + c] + TIME_STEP * (total[c] + extra) / ext[7]
            ext[4 + c] = moved
            ext[c] = ext[c] + TIME_STEP * moved

    for tile in range(tiles):
        span = pl.ds(tile * LANES, LANES)
        for c in range(3):
            positions_out[c : c + 1, span] = ext[c, tile + 1 : tile + 2, :]
            velocities_out[c : c + 1, span] = ext[4 + c, tile + 1 : tile + 2, :]


def body(
    positions,
    velocities,
    masses,
    atom_kinds,
    frag_atoms,
    assign,
    embed_table,
    neigh_table,
    w_query,
    w_key,
    w_value,
    w_energy,
    w_force,
    head_decay,
):
    tiles = positions.shape[1] // LANES
    slots, atoms = frag_atoms.shape
    heads = head_decay.shape[0]
    width = w_query.shape[0]
    ext_rows = -(-(tiles + 3) // 8) * 8
    vmem = pl.BlockSpec(memory_space=pltpu.VMEM)
    smem = pl.BlockSpec(memory_space=pltpu.SMEM)
    return pl.pallas_call(
        functools.partial(kernel, tiles, slots, heads),
        out_shape=(
            jax.ShapeDtypeStruct(positions.shape, F32),
            jax.ShapeDtypeStruct(velocities.shape, F32),
            jax.ShapeDtypeStruct((STEPS, slots), F32),
        ),
        in_specs=[vmem] * 13 + [smem],
        out_specs=(vmem, vmem, vmem),
        scratch_shapes=[
            pltpu.VMEM((8, ext_rows, LANES), F32),
            pltpu.VMEM((STEPS + 1, 2, 8, LANES), F32),
            pltpu.VMEM((STEPS + 1, 2, 8, LANES), F32),
            pltpu.VMEM((LANES, 2 * width), F32),
            pltpu.VMEM((width, LANES), F32),
            pltpu.VMEM((3, slots, LANES), F32),
            pltpu.VMEM((atoms, LANES), F32),
            pltpu.VMEM((slots, LANES), F32),
            pltpu.VMEM((slots * atoms, 2 * width), BF16),
            pltpu.VMEM((slots, 8, LANES), F32),
            pltpu.VMEM((slots, LANES), F32),
            pltpu.SemaphoreType.DMA((STEPS + 1, 2)),
            pltpu.SemaphoreType.DMA((STEPS + 1, 2)),
        ],
        compiler_params=pltpu.CompilerParams(
            collective_id=0, has_side_effects=True, vmem_limit_bytes=40 * 1024 * 1024
        ),
    )(
        positions,
        velocities,
        masses.reshape(tiles, LANES),
        atom_kinds.reshape(tiles, LANES),
        frag_atoms,
        assign,
        embed_table,
        neigh_table,
        w_query,
        w_key,
        w_value,
        w_energy.reshape(1, width),
        w_force,
        head_decay,
    )


def solution(mesh):
    both = ("dom", "grp")
    return jax.shard_map(
        body,
        mesh=mesh,
        in_specs=(
            P(None, both),
            P(None, both),
            P(both),
            P(both),
            P(both, None),
            P(None, both),
        )
        + (P(),) * 8,
        out_specs=(P(None, both), P(None, both), P(None, both)),
        check_vma=False,
    )
```

```python
import functools
import math

import jax
import jax.numpy as jnp
from jax import lax
from jax.experimental import pallas as pl
from jax.experimental.pallas import tpu as pltpu
from jax.sharding import PartitionSpec as P

HALO = 64
STEPS = 2
TIME_STEP = 0.05
NEAR_RATE = 0.5
FAR = 1e30
LANES = 128
UNROLL = 4
OPERANDS = 14
LOG2E = math.log2(math.e)
F32 = jnp.float32
BF16 = jnp.bfloat16


def dot_nn(a, b):
    return lax.dot_general(a, b, (((1,), (0,)), ((), ())), preferred_element_type=F32)


def dot_nt(a, b):
    return lax.dot_general(a, b, (((1,), (1,)), ((), ())), preferred_element_type=F32)


def lane_pick(x, index):
    return jnp.take_along_axis(x, index, axis=1, mode="promise_in_bounds")


def iota(shape, dim):
    return lax.broadcasted_iota(jnp.int32, shape, dim)


def to_row(column):
    size = column.shape[0]
    same = iota((size, size), 0) == iota((size, size), 1)
    return jnp.sum(jnp.where(same, column, 0.0), axis=0, keepdims=True)


def to_column(row):
    size = row.shape[1]
    same = iota((size, size), 0) == iota((size, size), 1)
    return jnp.sum(jnp.where(same, row, 0.0), axis=1, keepdims=True)


def silu_of_double(half):
    return half + half * jnp.tanh(half)


def kernel(tiles, slots, heads, *refs):
    operands, refs = refs[:OPERANDS], refs[OPERANDS:]
    (positions_out, velocities_out, energies_out), refs = refs[:3], refs[3:]
    local, refs = refs[:OPERANDS], refs[OPERANDS:]
    (
        ext,
        rim_out,
        rim_in,
        rows,
        cols,
        counts,
        spots,
        own_rows,
        neigh_rows,
        projections,
        head_readout,
        pulls,
        atom_energy,
        load_sem,
        send_sem,
        recv_sem,
    ) = refs
    loads = [
        pltpu.make_async_copy(source, target, load_sem.at[k])
        for k, (source, target) in enumerate(zip(operands, local))
    ]
    for load in loads:
        load.start()
    (
        positions,
        velocities,
        masses,
        kinds,
        frag_atoms,
        assign,
        embed,
        neigh,
        w_query,
        w_key,
        w_value,
        w_energy,
        w_force,
        head_decay,
    ) = local
    doms = lax.axis_size("dom")
    me = lax.axis_index("dom")
    upper, lower = lax.rem(me + 1, doms), lax.rem(me + doms - 1, doms)
    width = w_query.shape[0]
    head_width = width // heads
    ext_rows = ext.shape[1]
    types = embed.shape[0]

    barrier = pltpu.get_barrier_semaphore()
    for neighbour in (lower, upper):
        pl.semaphore_signal(
            barrier, inc=1, device_id={"dom": neighbour}, device_id_type=pl.DeviceIdType.MESH
        )

    lane = iota((slots, LANES), 1)

    for load in loads[:4]:
        load.wait()
    for tile in range(tiles):
        span = pl.ds(tile * LANES, LANES)
        for c in range(3):
            ext[c, tile + 1 : tile + 2, :] = positions[c : c + 1, span]
            ext[4 + c, tile + 1 : tile + 2, :] = velocities[c : c + 1, span]
    ext[3, 1 : tiles + 1, :] = kinds[...].astype(F32)
    ext[7, 1 : tiles + 1, :] = masses[...]
    for c in range(8):
        ext[c, tiles + 2 : ext_rows, :] = jnp.full((ext_rows - tiles - 2, LANES), 1.0, F32)
    for side, row in ((0, tiles), (1, 1)):
        for c in range(8):
            rim_out[0, side, c : c + 1, :] = ext[c, row : row + 1, :]

    def exchange(phase):
        copies = []
        for side, target in ((0, upper), (1, lower)):
            copy = pltpu.make_async_remote_copy(
                src_ref=rim_out.at[phase, side],
                dst_ref=rim_in.at[phase, side],
                send_sem=send_sem.at[phase, side],
                recv_sem=recv_sem.at[phase, side],
                device_id={"dom": target},
                device_id_type=pl.DeviceIdType.MESH,
            )
            copy.start()
            copies.append(copy)
        return copies

    pl.semaphore_wait(barrier, 2)
    copies = exchange(0)

    for load in loads[4:]:
        load.wait()
    readout = jnp.concatenate(
        [
            w_force[...],
            w_energy[...],
            jnp.zeros((15 - heads, width), F32),
        ],
        axis=0,
    )
    readout_hi = readout.astype(BF16).astype(F32)
    readout_lo = readout - readout_hi
    atoms = frag_atoms.shape[1]
    pairs = slots // 2
    projections[0:width] = jnp.transpose(w_key[...].astype(F32)).astype(BF16)
    projections[width : 2 * width] = jnp.transpose(w_value[...].astype(F32)).astype(BF16)
    projections[2 * width : 2 * width + 16] = readout_hi.astype(BF16)
    projections[2 * width + 16 : 2 * width + 32] = readout_lo.astype(BF16)
    feature_head = lax.shift_right_logical(iota((16, width), 1), 5)
    for h in range(heads):
        high, low = 16 * h, 16 * (heads + h)
        own = feature_head == h
        head_readout[high : high + 16] = jnp.where(own, readout_hi, 0.0).astype(BF16)
        head_readout[low : low + 16] = jnp.where(own, readout_lo, 0.0).astype(BF16)

    index = frag_atoms[...]
    live = jnp.where(index >= 0, 1.0, 0.0)
    active = to_column(jnp.where(assign[0:1, :] >= 0, 1.0, 0.0))
    count = jnp.sum(live, axis=1, keepdims=True) * active
    left_rows = iota((pairs, LANES), 1) < atoms
    counts[...] = jnp.where(left_rows, count[0:pairs], count[pairs:])
    start = jnp.maximum(index[:, 0:1], 0) + HALO
    tile_of = lax.shift_right_logical(start, 7)
    shift = jnp.bitwise_and(start, 127)
    both = jnp.concatenate([tile_of, tile_of + 1], axis=0)
    pick = jnp.where(iota((2 * slots, ext_rows), 1) == both, 1.0, 0.0)
    pick = jnp.concatenate([pick, pick, pick], axis=1).astype(BF16)
    put = jnp.where(
        iota((ext_rows, 2 * slots), 0).astype(F32) == to_row(both.astype(F32)), 1.0, 0.0
    )
    put = jnp.concatenate([put, put], axis=1).astype(BF16)
    half_lane = jnp.bitwise_and(lane, atoms - 1)
    ahead = half_lane + shift
    pick_lane = jnp.bitwise_and(ahead, 127)
    pick_first = ahead < LANES
    second = jnp.where(iota((slots, LANES), 0) < pairs, 0, atoms)
    put_lane = jnp.bitwise_and(lane - shift + second, 127)
    put_first = lane >= shift

    sub8 = iota((8, LANES), 0)
    lane8 = iota((8, LANES), 1)
    lane64 = iota((atoms, LANES), 1)
    sub64 = iota((atoms, LANES), 0)
    left8 = lane8 < atoms
    left16 = iota((16, LANES), 1) < atoms
    left64 = lane64 < atoms
    other = jnp.bitwise_and(lane64, atoms - 1)
    latest = jnp.maximum(sub64, other).astype(F32)
    distinct = sub64 != other
    member = jnp.where(left64, 0, pairs)
    keep_left = jnp.where(left64, 1.0, 0.0).astype(BF16)
    keep_right = jnp.where(left64, 0.0, 1.0).astype(BF16)
    per_group = LANES // head_width
    groups = heads // per_group
    half_scale = 0.5 / math.sqrt(head_width)
    decay_rows = [
        -LOG2E * jnp.where(left8[0:1], head_decay[:, 2 * t : 2 * t + 1], head_decay[:, 2 * t + 1 : 2 * t + 2])
        for t in range(heads // 2)
    ]
    flat_masks = [
        jnp.where(sub8 == 2 * t + jnp.where(left8, 0, 1), 1.0, 0.0) for t in range(heads // 2)
    ]
    empty = jnp.zeros((head_width, LANES), BF16)

    for copy in copies:
        copy.wait()
    for side, row in ((0, 0), (1, tiles + 1)):
        for c in range(8):
            ext[c, row : row + 1, :] = rim_in[0, side, c : c + 1, :]

    def gather(components):
        field = jnp.concatenate([ext[c] for c in components], axis=1)
        high = field.astype(BF16)
        rest = field - high.astype(F32)
        middle = rest.astype(BF16)
        low = (rest - middle.astype(F32)).astype(BF16)
        picked = dot_nn(pick, jnp.concatenate([high, middle, low], axis=0))
        result = []
        for c in range(len(components)):
            span = slice(c * LANES, (c + 1) * LANES)
            result.append(
                jnp.where(
                    pick_first,
                    lane_pick(picked[0:slots, span], pick_lane),
                    lane_pick(picked[slots:, span], pick_lane),
                )
            )
        return result

    def model(group, carry):
        first = group * (2 * UNROLL)
        mine = [first + k for k in range(2 * UNROLL)]
        many = range(2 * UNROLL)
        far, hidden = [], []
        for k in many:
            squared = None
            for c in range(3):
                column = lane_pick(cols[...], member + (c * slots + mine[k]))
                spread = column - rows[c, pl.ds(mine[k], 1), :]
                squared = spread * spread if squared is None else squared + spread * spread
            far.append(jnp.where(latest < counts[pl.ds(mine[k], 1), :], squared, FAR))
        summed = []
        for k in many:
            nearby = jnp.where(distinct, jnp.exp2((-NEAR_RATE * LOG2E) * far[k]), 0.0)
            near_hi = nearby.astype(BF16)
            near_lo = (nearby - near_hi.astype(F32)).astype(BF16)
            block = jnp.concatenate(
                [
                    jnp.concatenate([near * keep_left, near * keep_right], axis=0)
                    for near in (near_hi, near_lo)
                ],
                axis=1,
            )
            span = pl.ds(pl.multiple_of(mine[k] * LANES, LANES), LANES)
            theirs = neigh_rows[span, :]
            summed.append(dot_nn(block, jnp.concatenate([theirs, theirs], axis=0)))
        for k in many:
            span = pl.ds(pl.multiple_of(mine[k] * LANES, LANES), LANES)
            hidden.append(silu_of_double(summed[k] + own_rows[span, :]).astype(BF16))
        query, key, value, base = [], [], [], []
        for u in range(UNROLL):
            block = jnp.concatenate(hidden[2 * u : 2 * u + 2], axis=0)
            query.append(dot_nn(block, w_query[...]).astype(BF16))
            across = dot_nt(projections[...], block)
            key.append(across[0:width].astype(BF16))
            value.append(across[width : 2 * width].astype(BF16))
            base.append(across[2 * width : 2 * width + 16] + across[2 * width + 16 :])
        reads = [dot_nn(head_readout[...], value[u]) for u in range(UNROLL)]
        reads = [read[0 : 16 * heads] + read[16 * heads :] for read in reads]

        def scores(k):
            u, span = k // 2, slice((k % 2) * LANES, (k % 2 + 1) * LANES)
            straight = key[u][:, span]
            turned = pltpu.roll(straight, atoms, 1)
            result = []
            for m in range(2):
                at = (2 * (k % 2) + m) * atoms
                parts = []
                for g in range(groups):
                    blocks = []
                    for h in range(per_group):
                        feature = slice(
                            g * LANES + h * head_width, g * LANES + (h + 1) * head_width
                        )
                        source = straight if h % 2 == m else turned
                        keep = keep_left if h % 2 == 0 else keep_right
                        piece = source[feature] * keep[0:head_width]
                        blocks.append(
                            jnp.concatenate(
                                [piece if t == h // 2 else empty for t in range(per_group // 2)],
                                axis=1,
                            )
                        )
                    parts.append(
                        dot_nn(
                            query[u][at : at + atoms, g * LANES : (g + 1) * LANES],
                            jnp.concatenate(blocks, axis=0),
                        )
                    )
                result.append(parts)
            return result

        def weigh(k, parts):
            turned = pltpu.roll(far[k], atoms, 1)
            result = []
            for m in range(2):
                here = jnp.where(left64, far[k], turned) if m == 0 else jnp.where(left64, turned, far[k])
                tiles_out = []
                for t in range(heads // 2):
                    part = parts[m][t // 2][:, (t % 2) * LANES : (t % 2 + 1) * LANES]
                    envelope = jnp.exp2(here * decay_rows[t])
                    tiles_out.append((silu_of_double(part * half_scale) * envelope).astype(BF16))
                result.append(jnp.concatenate(tiles_out, axis=1))
            return jnp.concatenate(result, axis=0)

        weights = []
        ahead_scores = scores(0)
        for k in many:
            now = ahead_scores
            if k + 1 < 2 * UNROLL:
                ahead_scores = scores(k + 1)
            weights.append(weigh(k, now))
        mixed = []
        for k in many:
            u, span = k // 2, slice((k % 2) * LANES, (k % 2 + 1) * LANES)
            straight = reads[u][:, span]
            turned = pltpu.roll(straight, atoms, 1)
            left = []
            for m in range(2):
                a, b = (straight, turned) if m == 0 else (turned, straight)
                left.append(
                    jnp.concatenate(
                        [
                            jnp.where(
                                left16,
                                a[32 * t : 32 * t + 16],
                                b[32 * t + 16 : 32 * t + 32],
                            )
                            for t in range(heads // 2)
                        ],
                        axis=1,
                    )
                )
            left = jnp.concatenate(left, axis=0)
            left_hi = left.astype(BF16)
            left_lo = (left - left_hi.astype(F32)).astype(BF16)
            product = dot_nt(jnp.concatenate([left_hi, left_lo], axis=0), weights[k])
            mixed.append(product[0:32] + product[32:64])
        lefts = []
        for k in many:
            u, span = k // 2, slice((k % 2) * LANES, (k % 2 + 1) * LANES)
            scalars = jnp.where(left16, mixed[k][0:16], mixed[k][16:32]) + base[u][:, span]
            atom_energy[pl.ds(mine[k], 1), :] = scalars[heads : heads + 1]
            straight = scalars[0:heads]
            turned = pltpu.roll(straight, atoms, 1)
            left = []
            for m in range(2):
                a, b = (straight, turned) if m == 0 else (turned, straight)
                here = jnp.where(left8, a, b)
                place = spots[m * pairs + mine[k]]
                terms = []
                for t in range(heads // 2):
                    term = jnp.sum(here * flat_masks[t], axis=0, keepdims=True) * place
                    term_hi = term.astype(BF16).astype(F32)
                    terms.append(jnp.where(sub8 < 4, term_hi, term - term_hi))
                left.append(jnp.concatenate(terms, axis=1))
            lefts.append(jnp.concatenate(left, axis=0).astype(BF16))
        for k in many:
            pulled = dot_nt(lefts[k], weights[k])
            pulls[mine[k]] = jnp.where(left8, pulled[0:8], pulled[8:16])
        return carry

    for step in range(STEPS):
        fields = gather((0, 1, 2, 3) if step == 0 else (0, 1, 2))
        centred = [field - field[:, 0:1] for field in fields[:3]]
        for c in range(3):
            rows[c] = jnp.where(left_rows, centred[c][0:pairs], centred[c][pairs:])
            spots[:, c + 1, :] = centred[c]
            spots[:, c + 5, :] = centred[c]
        if step == 0:
            spots[:, 0, :] = jnp.ones((slots, LANES), F32)
            spots[:, 4, :] = jnp.ones((slots, LANES), F32)
            sort = jnp.where(half_lane.astype(F32) < count, fields[3], -1.0)
        else:
            sort = centred[0]
        cols[...] = jnp.transpose(jnp.concatenate(centred + [sort], axis=0))[0:atoms]
        if step == 0:
            both_tables = jnp.concatenate([embed[...] * 0.5, neigh[...] * 0.5], axis=1).astype(BF16)

            def look_up(group, carry):
                hot = []
                for k in range(2 * UNROLL):
                    for m in range(2):
                        at = 3 * slots + m * pairs + group * (2 * UNROLL) + k
                        kind = lane_pick(cols[...], jnp.full((atoms, LANES), at, jnp.int32))
                        hot.append(jnp.where(kind == lane64.astype(F32), 1.0, 0.0))
                hot = jnp.concatenate(hot, axis=0).astype(BF16)[:, 0:types]
                found = dot_nn(hot, both_tables)
                size = 2 * UNROLL * LANES
                span = pl.ds(pl.multiple_of(group * size, size), size)
                own_rows[span, :] = found[:, 0:width]
                neigh_rows[span, :] = found[:, width:].astype(BF16)
                return carry

            lax.fori_loop(0, pairs // (2 * UNROLL), look_up, 0)
        lax.fori_loop(0, pairs // (2 * UNROLL), model, 0)

        each = atom_energy[...]
        energy = jnp.concatenate(
            [
                jnp.sum(jnp.where(left_rows, each, 0.0), axis=1, keepdims=True),
                jnp.sum(jnp.where(left_rows, 0.0, each), axis=1, keepdims=True),
            ],
            axis=0,
        )
        energies_out[step : step + 1, :] = to_row(energy)
        sums = [pulls[:, q, :] + pulls[:, q + 4, :] for q in range(4)]
        firsts, seconds = [], []
        for c in range(3):
            force = rows[c] * sums[0] - sums[c + 1]
            force = jnp.concatenate(
                [jnp.where(left_rows, force, 0.0), jnp.where(left_rows, 0.0, force)], axis=0
            )
            turned = lane_pick(force, put_lane)
            firsts.append(jnp.where(put_first, turned, 0.0))
            seconds.append(jnp.where(put_first, 0.0, turned))
        placed = jnp.concatenate(
            [jnp.concatenate(firsts, axis=1), jnp.concatenate(seconds, axis=1)], axis=0
        )
        placed_hi = placed.astype(BF16)
        placed_lo = (placed - placed_hi.astype(F32)).astype(BF16)
        total = dot_nn(put, jnp.concatenate([placed_hi, placed_lo], axis=0))
        total = [total[:, c * LANES : (c + 1) * LANES] for c in range(3)]

        phase = step + 1
        for c in range(3):
            rim_out[phase, 0, c : c + 1, :] = total[c][tiles + 1 : tiles + 2]
            rim_out[phase, 0, c + 3 : c + 4, :] = total[c][tiles : tiles + 1]
            rim_out[phase, 1, c : c + 1, :] = total[c][0:1]
            rim_out[phase, 1, c + 3 : c + 4, :] = total[c][1:2]
        for side in range(2):
            rim_out[phase, side, 6:8, :] = jnp.zeros((2, LANES), F32)
        copies = exchange(phase)
        row_id = iota((ext_rows, LANES), 0)
        lane_id = iota((ext_rows, LANES), 1)
        from_lower = lane_id < HALO
        from_upper = lane_id >= LANES - HALO
        for copy in copies:
            copy.wait()
        for c in range(3):
            low = rim_in[phase, 0, c : c + 1, :]
            low_own = rim_in[phase, 0, c + 3 : c + 4, :]
            high = rim_in[phase, 1, c : c + 1, :]
            high_own = rim_in[phase, 1, c + 3 : c + 4, :]
            extra = jnp.where((row_id == 1) & from_lower, low, 0.0)
            extra = jnp.where((row_id == tiles) & from_upper, high, extra)
            extra = jnp.where((row_id == 0) & from_upper, low_own, extra)
            extra = jnp.where((row_id == tiles + 1) & from_lower, high_own, extra)
            moved = ext[4 + c] + TIME_STEP * (total[c] + extra) / ext[7]
            ext[4 + c] = moved
            ext[c] = ext[c] + TIME_STEP * moved

    for tile in range(tiles):
        span = pl.ds(tile * LANES, LANES)
        for c in range(3):
            positions_out[c : c + 1, span] = ext[c, tile + 1 : tile + 2, :]
            velocities_out[c : c + 1, span] = ext[4 + c, tile + 1 : tile + 2, :]


def hand_over(*refs):
    for k in range(3):
        refs[k + 3][...] = refs[k][...]


def body(
    positions,
    velocities,
    masses,
    atom_kinds,
    frag_atoms,
    assign,
    embed_table,
    neigh_table,
    w_query,
    w_key,
    w_value,
    w_energy,
    w_force,
    head_decay,
):
    tiles = positions.shape[1] // LANES
    slots, atoms = frag_atoms.shape
    heads = head_decay.shape[0]
    width = w_query.shape[0]
    ext_rows = -(-(tiles + 3) // 8) * 8
    vmem = pl.BlockSpec(memory_space=pltpu.VMEM)
    operands = (
        positions,
        velocities,
        masses.reshape(tiles, LANES),
        atom_kinds.reshape(tiles, LANES),
        frag_atoms,
        assign,
        embed_table,
        neigh_table,
        w_query,
        w_key,
        w_value,
        w_energy.reshape(1, width),
        w_force.T,
        head_decay.reshape(1, heads),
    )
    results = pl.pallas_call(
        functools.partial(kernel, tiles, slots, heads),
        out_shape=(
            jax.ShapeDtypeStruct(positions.shape, F32),
            jax.ShapeDtypeStruct(velocities.shape, F32),
            jax.ShapeDtypeStruct((STEPS, slots), F32),
        ),
        in_specs=[pl.BlockSpec(memory_space=pltpu.HBM)] * OPERANDS,
        out_specs=(vmem, vmem, vmem),
        scratch_shapes=[pltpu.VMEM(operand.shape, operand.dtype) for operand in operands]
        + [
            pltpu.VMEM((8, ext_rows, LANES), F32),
            pltpu.VMEM((STEPS + 1, 2, 8, LANES), F32),
            pltpu.VMEM((STEPS + 1, 2, 8, LANES), F32),
            pltpu.VMEM((3, slots // 2, LANES), F32),
            pltpu.VMEM((atoms, LANES), F32),
            pltpu.VMEM((slots // 2, LANES), F32),
            pltpu.VMEM((slots, 8, LANES), F32),
            pltpu.VMEM((slots * atoms, width), F32),
            pltpu.VMEM((slots * atoms, width), BF16),
            pltpu.VMEM((2 * width + 32, width), BF16),
            pltpu.VMEM((32 * heads, width), BF16),
            pltpu.VMEM((slots // 2, 8, LANES), F32),
            pltpu.VMEM((slots // 2, LANES), F32),
            pltpu.SemaphoreType.DMA((OPERANDS,)),
            pltpu.SemaphoreType.DMA((STEPS + 1, 2)),
            pltpu.SemaphoreType.DMA((STEPS + 1, 2)),
        ],
        compiler_params=pltpu.CompilerParams(
            collective_id=0, has_side_effects=True, vmem_limit_bytes=56 * 1024 * 1024
        ),
    )(*operands)
    return pl.pallas_call(
        hand_over,
        out_shape=tuple(jax.ShapeDtypeStruct(result.shape, F32) for result in results),
        in_specs=[vmem] * 3,
        out_specs=(vmem,) * 3,
        compiler_params=pltpu.CompilerParams(vmem_limit_bytes=56 * 1024 * 1024),
    )(*results)


def solution(mesh):
    both = ("dom", "grp")
    return jax.shard_map(
        body,
        mesh=mesh,
        in_specs=(
            P(None, both),
            P(None, both),
            P(both),
            P(both),
            P(both, None),
            P(None, both),
        )
        + (P(),) * 8,
        out_specs=(P(None, both), P(None, both), P(None, both)),
        check_vma=False,
    )
```

```python
import functools
import math

import jax
import jax.numpy as jnp
from jax import lax
from jax.experimental import pallas as pl
from jax.experimental.pallas import tpu as pltpu
from jax.sharding import PartitionSpec as P

HALO = 64
STEPS = 2
TIME_STEP = 0.05
NEAR_RATE = 0.5
FAR = 1e30
LANES = 128
TERMS = 24
OPERANDS = 14
F32 = jnp.float32
BF16 = jnp.bfloat16


def dot_nn(a, b):
    return lax.dot_general(a, b, (((1,), (0,)), ((), ())), preferred_element_type=F32)


def dot_nt(a, b):
    return lax.dot_general(a, b, (((1,), (1,)), ((), ())), preferred_element_type=F32)


def lane_pick(x, index):
    return jnp.take_along_axis(x, index, axis=1, mode="promise_in_bounds")


def iota(shape, dim):
    return lax.broadcasted_iota(jnp.int32, shape, dim)


def to_row(column):
    size = column.shape[0]
    same = iota((size, size), 0) == iota((size, size), 1)
    return jnp.sum(jnp.where(same, column, 0.0), axis=0, keepdims=True)


def to_column(row):
    size = row.shape[1]
    same = iota((size, size), 0) == iota((size, size), 1)
    return jnp.sum(jnp.where(same, row, 0.0), axis=1, keepdims=True)


def silu_of_double(half):
    return half + half * jnp.tanh(half)


def kernel(tiles, slots, heads, *refs):
    operands, refs = refs[:OPERANDS], refs[OPERANDS:]
    (positions_out, velocities_out, energies_out), refs = refs[:3], refs[3:]
    local, refs = refs[:OPERANDS], refs[OPERANDS:]
    (
        ext,
        rim_out,
        rim_in,
        rows,
        cols,
        counts,
        spots,
        own_rows,
        neigh_rows,
        projections,
        head_readout,
        pulls,
        atom_energy,
        firsts,
        seconds,
        load_sem,
        send_sem,
        recv_sem,
    ) = refs
    loads = [
        pltpu.make_async_copy(source, target, load_sem.at[k])
        for k, (source, target) in enumerate(zip(operands, local))
    ]
    for load in loads:
        load.start()
    (
        positions,
        velocities,
        masses,
        kinds,
        frag_atoms,
        assign,
        embed,
        neigh,
        w_query,
        w_key,
        w_value,
        w_energy,
        w_force,
        head_decay,
    ) = local
    doms = lax.axis_size("dom")
    me = lax.axis_index("dom")
    upper, lower = lax.rem(me + 1, doms), lax.rem(me + doms - 1, doms)
    width = w_query.shape[0]
    head_width = width // heads
    ext_rows = ext.shape[1]
    types = embed.shape[0]

    barrier = pltpu.get_barrier_semaphore()
    for neighbour in (lower, upper):
        pl.semaphore_signal(
            barrier, inc=1, device_id={"dom": neighbour}, device_id_type=pl.DeviceIdType.MESH
        )

    lane = iota((slots, LANES), 1)

    for load in loads[:4]:
        load.wait()
    for side, tile in ((0, tiles - 1), (1, 0)):
        span = pl.ds(tile * LANES, LANES)
        rim_out[0, side, 0:3, :] = positions[:, span]
        rim_out[0, side, 3:4, :] = kinds[tile : tile + 1, :].astype(F32)
        rim_out[0, side, 4:7, :] = velocities[:, span]
        rim_out[0, side, 7:8, :] = masses[tile : tile + 1, :]

    def exchange(phase):
        copies = []
        for side, target in ((0, upper), (1, lower)):
            copy = pltpu.make_async_remote_copy(
                src_ref=rim_out.at[phase, side],
                dst_ref=rim_in.at[phase, side],
                send_sem=send_sem.at[phase, side],
                recv_sem=recv_sem.at[phase, side],
                device_id={"dom": target},
                device_id_type=pl.DeviceIdType.MESH,
            )
            copy.start()
            copies.append(copy)
        return copies

    pl.semaphore_wait(barrier, 2)
    copies = exchange(0)

    for tile in range(tiles):
        span = pl.ds(tile * LANES, LANES)
        for c in range(3):
            ext[c, tile + 1 : tile + 2, :] = positions[c : c + 1, span]
            ext[4 + c, tile + 1 : tile + 2, :] = velocities[c : c + 1, span]
    ext[3, 1 : tiles + 1, :] = kinds[...].astype(F32)
    ext[7, 1 : tiles + 1, :] = masses[...]
    for c in range(8):
        ext[c, tiles + 2 : ext_rows, :] = jnp.full((ext_rows - tiles - 2, LANES), 1.0, F32)
    for phase in range(1, STEPS + 1):
        for side in range(2):
            rim_out[phase, side, 6:8, :] = jnp.zeros((2, LANES), F32)

    for load in loads[4:]:
        load.wait()
    readout = jnp.concatenate(
        [
            w_force[...],
            w_energy[...],
            jnp.zeros((15 - heads, width), F32),
        ],
        axis=0,
    )
    readout_hi = readout.astype(BF16).astype(F32)
    readout_lo = readout - readout_hi
    atoms = frag_atoms.shape[1]
    pairs = slots // 2
    projections[0:width] = jnp.transpose(w_key[...].astype(F32)).astype(BF16)
    projections[width : 2 * width] = jnp.transpose(w_value[...].astype(F32)).astype(BF16)
    projections[2 * width : 2 * width + 16] = readout_hi.astype(BF16)
    projections[2 * width + 16 : 2 * width + 32] = readout_lo.astype(BF16)
    feature_head = lax.shift_right_logical(iota((16, width), 1), 5)
    for h in range(heads):
        high, low = 16 * h, 16 * (heads + h)
        own = feature_head == h
        head_readout[high : high + 16] = jnp.where(own, readout_hi, 0.0).astype(BF16)
        head_readout[low : low + 16] = jnp.where(own, readout_lo, 0.0).astype(BF16)

    index = frag_atoms[...]
    live = jnp.where(index >= 0, 1.0, 0.0)
    active = to_column(jnp.where(assign[0:1, :] >= 0, 1.0, 0.0))
    count = jnp.sum(live, axis=1, keepdims=True) * active
    left_rows = iota((pairs, LANES), 1) < atoms
    counts[...] = jnp.where(left_rows, count[0:pairs], count[pairs:])
    start = jnp.maximum(index[:, 0:1], 0) + HALO
    tile_of = lax.shift_right_logical(start, 7)
    shift = jnp.bitwise_and(start, 127)
    both = jnp.concatenate([tile_of, tile_of + 1], axis=0)
    pick = jnp.where(iota((2 * slots, ext_rows), 1) == both, 1.0, 0.0)
    pick = jnp.concatenate([pick, pick, pick], axis=1).astype(BF16)
    put = jnp.where(
        iota((ext_rows, 2 * slots), 0).astype(F32) == to_row(both.astype(F32)), 1.0, 0.0
    )
    put = jnp.concatenate([put, put], axis=1).astype(BF16)
    half_lane = jnp.bitwise_and(lane, atoms - 1)
    ahead = half_lane + shift
    pick_lane = jnp.bitwise_and(ahead, 127)
    pick_first = ahead < LANES
    second = jnp.where(iota((slots, LANES), 0) < pairs, 0, atoms)
    put_lane = jnp.bitwise_and(lane - shift + second, 127)
    put_first = lane >= shift

    sub8 = iota((8, LANES), 0)
    lane8 = iota((8, LANES), 1)
    lane64 = iota((atoms, LANES), 1)
    sub64 = iota((atoms, LANES), 0)
    left8 = lane8 < atoms
    left16 = iota((16, LANES), 1) < atoms
    left64 = lane64 < atoms
    other = jnp.bitwise_and(lane64, atoms - 1)
    latest = jnp.maximum(sub64, other).astype(F32)
    distinct = sub64 != other
    keep_left = jnp.where(left64, 1.0, 0.0).astype(BF16)
    keep_right = jnp.where(left64, 0.0, 1.0).astype(BF16)
    per_group = LANES // head_width
    groups = heads // per_group
    half_scale = 0.5 / math.sqrt(head_width)
    decay_rows = [
        -jnp.where(left8[0:1], head_decay[:, 2 * t : 2 * t + 1], head_decay[:, 2 * t + 1 : 2 * t + 2])
        for t in range(heads // 2)
    ]
    flat_masks = [
        jnp.where(sub8 == 2 * t + jnp.where(left8, 0, 1), 1.0, 0.0) for t in range(heads // 2)
    ]
    empty = jnp.zeros((head_width, LANES), BF16)

    for copy in copies:
        copy.wait()
    for side, row in ((0, 0), (1, tiles + 1)):
        for c in range(8):
            ext[c, row : row + 1, :] = rim_in[0, side, c : c + 1, :]
    ext[7] = TIME_STEP / ext[7]
    shared = (iota((2, LANES), 0) == 0) == (iota((2, LANES), 1) >= HALO)

    def gather(components):
        field = jnp.concatenate([ext[c] for c in components], axis=1)
        high = field.astype(BF16)
        rest = field - high.astype(F32)
        middle = rest.astype(BF16)
        low = (rest - middle.astype(F32)).astype(BF16)
        picked = dot_nn(pick, jnp.concatenate([high, middle, low], axis=0))
        result = []
        for c in range(len(components)):
            span = slice(c * LANES, (c + 1) * LANES)
            result.append(
                jnp.where(
                    pick_first,
                    lane_pick(picked[0:slots, span], pick_lane),
                    lane_pick(picked[slots:, span], pick_lane),
                )
            )
        return result

    quads = pairs // 2
    many = range(pairs)
    nothing = jnp.zeros((2 * TERMS, LANES), BF16)

    def set_distances(centred):
        def parts(x):
            high = x.astype(BF16).astype(F32)
            middle = (x - high).astype(BF16).astype(F32)
            return high, middle, x - high - middle

        ones = jnp.ones((slots, LANES), F32)
        terms = []
        norm = None
        for x in centred:
            norm = x * x if norm is None else norm + x * x
            h, m, l = parts(x)
            terms += [(h, h), (h, m), (m, h), (h, l), (l, h), (m, m)]
        terms = [(-2.0 * a, b) for a, b in terms]
        for n in parts(norm):
            terms += [(n, ones), (ones, n)]
        for k, (a, b) in enumerate(terms):
            firsts[:, k, :] = a[0:pairs]
            firsts[:, TERMS + k, :] = a[pairs:]
            seconds[:, k, :] = jnp.where(left_rows, b[0:pairs], 0.0)
            seconds[:, TERMS + k, :] = jnp.where(left_rows, 0.0, b[pairs:])

    def model():
        far, hidden = [], []
        for u in range(quads):
            both = firsts[2 * u : 2 * u + 2].reshape(4 * TERMS, LANES)
            left = jnp.transpose(both)[0:atoms].astype(BF16)
            right = [seconds[2 * u + v].astype(BF16) for v in range(2)]
            right = jnp.concatenate(
                [
                    jnp.concatenate([right[0], nothing], axis=0),
                    jnp.concatenate([nothing, right[1]], axis=0),
                ],
                axis=1,
            )
            squared = dot_nn(left, right)
            for v in range(2):
                inside = latest < counts[2 * u + v : 2 * u + v + 1, :]
                far.append(jnp.where(inside, squared[:, v * LANES : (v + 1) * LANES], FAR))
        summed = []
        for k in many:
            nearby = jnp.where(distinct, jnp.exp(-NEAR_RATE * far[k]), 0.0)
            near_hi = nearby.astype(BF16)
            near_lo = (nearby - near_hi.astype(F32)).astype(BF16)
            block = jnp.concatenate(
                [
                    jnp.concatenate([near * keep_left, near * keep_right], axis=0)
                    for near in (near_hi, near_lo)
                ],
                axis=1,
            )
            span = slice(k * LANES, (k + 1) * LANES)
            theirs = neigh_rows[span, :]
            summed.append(dot_nn(block, jnp.concatenate([theirs, theirs], axis=0)))
        for k in many:
            span = slice(k * LANES, (k + 1) * LANES)
            hidden.append(silu_of_double(summed[k] + own_rows[span, :]).astype(BF16))
        query, key, value, base = [], [], [], []
        for u in range(quads):
            block = jnp.concatenate(hidden[2 * u : 2 * u + 2], axis=0)
            query.append(dot_nn(block, w_query[...]).astype(BF16))
            across = dot_nt(projections[...], block)
            key.append(across[0:width].astype(BF16))
            value.append(across[width : 2 * width].astype(BF16))
            base.append(across[2 * width : 2 * width + 16] + across[2 * width + 16 :])
        reads = [dot_nn(head_readout[...], value[u]) for u in range(quads)]
        reads = [read[0 : 16 * heads] + read[16 * heads :] for read in reads]

        def scores(k):
            u, span = k // 2, slice((k % 2) * LANES, (k % 2 + 1) * LANES)
            straight = key[u][:, span]
            turned = pltpu.roll(straight, atoms, 1)
            result = []
            for m in range(2):
                at = (2 * (k % 2) + m) * atoms
                parts = []
                for g in range(groups):
                    blocks = []
                    for h in range(per_group):
                        feature = slice(
                            g * LANES + h * head_width, g * LANES + (h + 1) * head_width
                        )
                        source = straight if h % 2 == m else turned
                        keep = keep_left if h % 2 == 0 else keep_right
                        piece = source[feature] * keep[0:head_width]
                        blocks.append(
                            jnp.concatenate(
                                [piece if t == h // 2 else empty for t in range(per_group // 2)],
                                axis=1,
                            )
                        )
                    parts.append(
                        dot_nn(
                            query[u][at : at + atoms, g * LANES : (g + 1) * LANES],
                            jnp.concatenate(blocks, axis=0),
                        )
                    )
                result.append(parts)
            return result

        def weigh(k, parts):
            turned = pltpu.roll(far[k], atoms, 1)
            result = []
            for m in range(2):
                here = jnp.where(left64, far[k], turned) if m == 0 else jnp.where(left64, turned, far[k])
                tiles_out = []
                for t in range(heads // 2):
                    part = parts[m][t // 2][:, (t % 2) * LANES : (t % 2 + 1) * LANES]
                    envelope = jnp.exp(here * decay_rows[t])
                    tiles_out.append((silu_of_double(part * half_scale) * envelope).astype(BF16))
                result.append(jnp.concatenate(tiles_out, axis=1))
            return jnp.concatenate(result, axis=0)

        weights = []
        ahead_scores = scores(0)
        for k in many:
            now = ahead_scores
            if k + 1 < pairs:
                ahead_scores = scores(k + 1)
            weights.append(weigh(k, now))
        mixed = []
        for k in many:
            u, span = k // 2, slice((k % 2) * LANES, (k % 2 + 1) * LANES)
            straight = reads[u][:, span]
            turned = pltpu.roll(straight, atoms, 1)
            left = []
            for m in range(2):
                a, b = (straight, turned) if m == 0 else (turned, straight)
                left.append(
                    jnp.concatenate(
                        [
                            jnp.where(
                                left16,
                                a[32 * t : 32 * t + 16],
                                b[32 * t + 16 : 32 * t + 32],
                            )
                            for t in range(heads // 2)
                        ],
                        axis=1,
                    )
                )
            left = jnp.concatenate(left, axis=0)
            left_hi = left.astype(BF16)
            left_lo = (left - left_hi.astype(F32)).astype(BF16)
            product = dot_nt(jnp.concatenate([left_hi, left_lo], axis=0), weights[k])
            mixed.append(product[0:32] + product[32:64])
        lefts = []
        for k in many:
            u, span = k // 2, slice((k % 2) * LANES, (k % 2 + 1) * LANES)
            scalars = jnp.where(left16, mixed[k][0:16], mixed[k][16:32]) + base[u][:, span]
            atom_energy[k : k + 1, :] = scalars[heads : heads + 1]
            straight = scalars[0:heads]
            turned = pltpu.roll(straight, atoms, 1)
            left = []
            for m in range(2):
                a, b = (straight, turned) if m == 0 else (turned, straight)
                here = jnp.where(left8, a, b)
                place = spots[m * pairs + k]
                terms = []
                for t in range(heads // 2):
                    term = jnp.sum(here * flat_masks[t], axis=0, keepdims=True) * place
                    term_hi = term.astype(BF16).astype(F32)
                    terms.append(jnp.where(sub8 < 4, term_hi, term - term_hi))
                left.append(jnp.concatenate(terms, axis=1))
            lefts.append(jnp.concatenate(left, axis=0).astype(BF16))
        for k in many:
            pulled = dot_nt(lefts[k], weights[k])
            pulls[k] = jnp.where(left8, pulled[0:8], pulled[8:16])

    def finish_energy(step):
        each = atom_energy[...]
        energy = jnp.concatenate(
            [
                jnp.sum(jnp.where(left_rows, each, 0.0), axis=1, keepdims=True),
                jnp.sum(jnp.where(left_rows, 0.0, each), axis=1, keepdims=True),
            ],
            axis=0,
        )
        energies_out[step : step + 1, :] = to_row(energy)

    def hand_out(which):
        for tile in which:
            span = pl.ds(tile * LANES, LANES)
            for c in range(3):
                positions_out[c : c + 1, span] = ext[c, tile + 1 : tile + 2, :]
                velocities_out[c : c + 1, span] = ext[4 + c, tile + 1 : tile + 2, :]

    for step in range(STEPS):
        fields = gather((0, 1, 2, 3) if step == 0 else (0, 1, 2))
        centred = [field - field[:, 0:1] for field in fields[:3]]
        for c in range(3):
            rows[c] = jnp.where(left_rows, centred[c][0:pairs], centred[c][pairs:])
            spots[:, c + 1, :] = centred[c]
            spots[:, c + 5, :] = centred[c]
        set_distances(centred)
        if step == 0:
            spots[:, 0, :] = jnp.ones((slots, LANES), F32)
            spots[:, 4, :] = jnp.ones((slots, LANES), F32)
            sort = jnp.where(half_lane.astype(F32) < count, fields[3], -1.0)
            cols[...] = jnp.transpose(jnp.concatenate([sort] * (LANES // slots), axis=0))[0:atoms]
            both_tables = jnp.concatenate([embed[...] * 0.5, neigh[...] * 0.5], axis=1).astype(BF16)

            for u in range(quads):
                hot = []
                for k in (2 * u, 2 * u + 1):
                    for m in range(2):
                        at = jnp.full((atoms, LANES), m * pairs + k, jnp.int32)
                        kind = lane_pick(cols[...], at)
                        hot.append(jnp.where(kind == lane64.astype(F32), 1.0, 0.0))
                hot = jnp.concatenate(hot, axis=0).astype(BF16)[:, 0:types]
                found = dot_nn(hot, both_tables)
                span = slice(2 * u * LANES, (2 * u + 2) * LANES)
                own_rows[span, :] = found[:, 0:width]
                neigh_rows[span, :] = found[:, width:].astype(BF16)
        model()

        sums = [pulls[:, q, :] + pulls[:, q + 4, :] for q in range(4)]
        placed_here, placed_next = [], []
        for c in range(3):
            force = rows[c] * sums[0] - sums[c + 1]
            force = jnp.concatenate(
                [jnp.where(left_rows, force, 0.0), jnp.where(left_rows, 0.0, force)], axis=0
            )
            turned = lane_pick(force, put_lane)
            placed_here.append(jnp.where(put_first, turned, 0.0))
            placed_next.append(jnp.where(put_first, 0.0, turned))
        placed = jnp.concatenate(
            [jnp.concatenate(placed_here, axis=1), jnp.concatenate(placed_next, axis=1)], axis=0
        )
        placed_hi = placed.astype(BF16)
        placed_lo = (placed - placed_hi.astype(F32)).astype(BF16)
        total = dot_nn(put, jnp.concatenate([placed_hi, placed_lo], axis=0))
        total = [total[:, c * LANES : (c + 1) * LANES] for c in range(3)]

        phase = step + 1
        for c in range(3):
            rim_out[phase, 0, 2 * c : 2 * c + 2, :] = total[c][tiles : tiles + 2]
            rim_out[phase, 1, 2 * c : 2 * c + 2, :] = total[c][0:2]
        copies = exchange(phase)
        for c in range(3):
            moved = ext[4 + c] + total[c] * ext[7]
            ext[4 + c] = moved
            ext[c] = ext[c] + TIME_STEP * moved
        finish_energy(step)
        if step == STEPS - 1:
            hand_out(range(1, tiles - 1))
        for copy in copies:
            copy.wait()
        for side, row in ((0, 0), (1, tiles)):
            border = slice(row, row + 2)
            for c in range(3):
                extra = jnp.where(shared, rim_in[phase, side, 2 * c : 2 * c + 2, :], 0.0)
                kick = extra * ext[7, border, :]
                ext[4 + c, border, :] = ext[4 + c, border, :] + kick
                ext[c, border, :] = ext[c, border, :] + TIME_STEP * kick
    hand_out((0, tiles - 1))


def hand_over(*refs):
    for k in range(3):
        refs[k + 3][...] = refs[k][...]


def body(
    positions,
    velocities,
    masses,
    atom_kinds,
    frag_atoms,
    assign,
    embed_table,
    neigh_table,
    w_query,
    w_key,
    w_value,
    w_energy,
    w_force,
    head_decay,
):
    tiles = positions.shape[1] // LANES
    slots, atoms = frag_atoms.shape
    heads = head_decay.shape[0]
    width = w_query.shape[0]
    ext_rows = -(-(tiles + 3) // 8) * 8
    vmem = pl.BlockSpec(memory_space=pltpu.VMEM)
    operands = (
        positions,
        velocities,
        masses.reshape(tiles, LANES),
        atom_kinds.reshape(tiles, LANES),
        frag_atoms,
        assign,
        embed_table,
        neigh_table,
        w_query,
        w_key,
        w_value,
        w_energy.reshape(1, width),
        w_force.T,
        head_decay.reshape(1, heads),
    )
    results = pl.pallas_call(
        functools.partial(kernel, tiles, slots, heads),
        out_shape=(
            jax.ShapeDtypeStruct(positions.shape, F32),
            jax.ShapeDtypeStruct(velocities.shape, F32),
            jax.ShapeDtypeStruct((STEPS, slots), F32),
        ),
        in_specs=[pl.BlockSpec(memory_space=pltpu.HBM)] * OPERANDS,
        out_specs=(vmem, vmem, vmem),
        scratch_shapes=[pltpu.VMEM(operand.shape, operand.dtype) for operand in operands]
        + [
            pltpu.VMEM((8, ext_rows, LANES), F32),
            pltpu.VMEM((STEPS + 1, 2, 8, LANES), F32),
            pltpu.VMEM((STEPS + 1, 2, 8, LANES), F32),
            pltpu.VMEM((3, slots // 2, LANES), F32),
            pltpu.VMEM((atoms, LANES), F32),
            pltpu.VMEM((slots // 2, LANES), F32),
            pltpu.VMEM((slots, 8, LANES), F32),
            pltpu.VMEM((slots * atoms, width), F32),
            pltpu.VMEM((slots * atoms, width), BF16),
            pltpu.VMEM((2 * width + 32, width), BF16),
            pltpu.VMEM((32 * heads, width), BF16),
            pltpu.VMEM((slots // 2, 8, LANES), F32),
            pltpu.VMEM((slots // 2, LANES), F32),
            pltpu.VMEM((slots // 2, 2 * TERMS, LANES), F32),
            pltpu.VMEM((slots // 2, 2 * TERMS, LANES), F32),
            pltpu.SemaphoreType.DMA((OPERANDS,)),
            pltpu.SemaphoreType.DMA((STEPS + 1, 2)),
            pltpu.SemaphoreType.DMA((STEPS + 1, 2)),
        ],
        compiler_params=pltpu.CompilerParams(
            collective_id=0, has_side_effects=True, vmem_limit_bytes=56 * 1024 * 1024
        ),
    )(*operands)
    return pl.pallas_call(
        hand_over,
        out_shape=tuple(jax.ShapeDtypeStruct(result.shape, F32) for result in results),
        in_specs=[vmem] * 3,
        out_specs=(vmem,) * 3,
        compiler_params=pltpu.CompilerParams(vmem_limit_bytes=56 * 1024 * 1024),
    )(*results)


def solution(mesh):
    both = ("dom", "grp")
    return jax.shard_map(
        body,
        mesh=mesh,
        in_specs=(
            P(None, both),
            P(None, both),
            P(both),
            P(both),
            P(both, None),
            P(None, both),
        )
        + (P(),) * 8,
        out_specs=(P(None, both), P(None, both), P(None, both)),
        check_vma=False,
    )
```

```python
import functools
import math

import jax
import jax.numpy as jnp
from jax import lax
from jax.experimental import pallas as pl
from jax.experimental.pallas import tpu as pltpu
from jax.sharding import PartitionSpec as P

HALO = 64
STEPS = 2
TIME_STEP = 0.05
NEAR_RATE = 0.5
FAR = 1e30
LANES = 128
OPERANDS = 14
F32 = jnp.float32
BF16 = jnp.bfloat16


def dot_nn(a, b):
    return lax.dot_general(a, b, (((1,), (0,)), ((), ())), preferred_element_type=F32)


def dot_nt(a, b):
    return lax.dot_general(a, b, (((1,), (1,)), ((), ())), preferred_element_type=F32)


def lane_pick(x, index):
    return jnp.take_along_axis(x, index, axis=1, mode="promise_in_bounds")


def iota(shape, dim):
    return lax.broadcasted_iota(jnp.int32, shape, dim)


def to_row(column):
    size = column.shape[0]
    same = iota((size, size), 0) == iota((size, size), 1)
    return jnp.sum(jnp.where(same, column, 0.0), axis=0, keepdims=True)


def to_column(row):
    size = row.shape[1]
    same = iota((size, size), 0) == iota((size, size), 1)
    return jnp.sum(jnp.where(same, row, 0.0), axis=1, keepdims=True)


def silu_of_double(half):
    return half + half * jnp.tanh(half)


def order_of_work(quads):
    many = range(2 * quads)
    order = [("project", u) for u in range(quads)] + [("read", u) for u in range(quads)]
    order.append(("score", 0))
    for k in many:
        if k + 1 in many:
            order.append(("score", k + 1))
        order.append(("weigh", k))
        if k - 2 in many:
            order.append(("mix", k - 2))
    order += [("mix", k) for k in many[-2:]]
    order += [("flatten", k) for k in many]
    order += [("pull", k) for k in many]
    return order


def kernel(tiles, slots, heads, *refs):
    operands, refs = refs[:OPERANDS], refs[OPERANDS:]
    (positions_out, velocities_out, energies_out), refs = refs[:3], refs[3:]
    local, refs = refs[:OPERANDS], refs[OPERANDS:]
    (
        ext,
        rim_out,
        rim_in,
        rows,
        cols,
        counts,
        places,
        own_rows,
        neigh_rows,
        projections,
        head_readout,
        pulls,
        atom_energy,
        load_sem,
        send_sem,
        recv_sem,
    ) = refs
    loads = [
        pltpu.make_async_copy(source, target, load_sem.at[k])
        for k, (source, target) in enumerate(zip(operands, local))
    ]
    for load in loads:
        load.start()
    (
        positions,
        velocities,
        masses,
        kinds,
        frag_atoms,
        assign,
        embed,
        neigh,
        w_query,
        w_key,
        w_value,
        w_energy,
        w_force,
        head_decay,
    ) = local
    doms = lax.axis_size("dom")
    me = lax.axis_index("dom")
    upper, lower = lax.rem(me + 1, doms), lax.rem(me + doms - 1, doms)
    width = w_query.shape[0]
    head_width = width // heads
    ext_rows = ext.shape[1]
    types = embed.shape[0]

    barrier = pltpu.get_barrier_semaphore()
    for neighbour in (lower, upper):
        pl.semaphore_signal(
            barrier, inc=1, device_id={"dom": neighbour}, device_id_type=pl.DeviceIdType.MESH
        )

    lane = iota((slots, LANES), 1)

    for load in loads[:4]:
        load.wait()
    for side, tile in ((0, tiles - 1), (1, 0)):
        span = pl.ds(tile * LANES, LANES)
        rim_out[0, side, 0:3, :] = positions[:, span]
        rim_out[0, side, 3:4, :] = kinds[tile : tile + 1, :].astype(F32)
        rim_out[0, side, 4:7, :] = velocities[:, span]
        rim_out[0, side, 7:8, :] = masses[tile : tile + 1, :]

    def exchange(phase):
        copies = []
        for side, target in ((0, upper), (1, lower)):
            copy = pltpu.make_async_remote_copy(
                src_ref=rim_out.at[phase, side],
                dst_ref=rim_in.at[phase, side],
                send_sem=send_sem.at[phase, side],
                recv_sem=recv_sem.at[phase, side],
                device_id={"dom": target},
                device_id_type=pl.DeviceIdType.MESH,
            )
            copy.start()
            copies.append(copy)
        return copies

    pl.semaphore_wait(barrier, 2)
    copies = exchange(0)

    for tile in range(tiles):
        span = pl.ds(tile * LANES, LANES)
        for c in range(3):
            ext[c, tile + 1 : tile + 2, :] = positions[c : c + 1, span]
            ext[4 + c, tile + 1 : tile + 2, :] = velocities[c : c + 1, span]
    ext[3, 1 : tiles + 1, :] = kinds[...].astype(F32)
    ext[7, 1 : tiles + 1, :] = masses[...]
    for c in range(8):
        ext[c, tiles + 2 : ext_rows, :] = jnp.full((ext_rows - tiles - 2, LANES), 1.0, F32)
    for phase in range(1, STEPS + 1):
        for side in range(2):
            rim_out[phase, side, 6:8, :] = jnp.zeros((2, LANES), F32)

    for load in loads[4:]:
        load.wait()
    readout = jnp.concatenate(
        [
            w_force[...],
            w_energy[...],
            jnp.zeros((15 - heads, width), F32),
        ],
        axis=0,
    )
    readout_hi = readout.astype(BF16).astype(F32)
    readout_lo = readout - readout_hi
    atoms = frag_atoms.shape[1]
    pairs = slots // 2
    projections[0:width] = jnp.transpose(w_key[...].astype(F32)).astype(BF16)
    projections[width : 2 * width] = jnp.transpose(w_value[...].astype(F32)).astype(BF16)
    projections[2 * width : 2 * width + 16] = readout_hi.astype(BF16)
    projections[2 * width + 16 : 2 * width + 32] = readout_lo.astype(BF16)
    feature_head = lax.shift_right_logical(iota((16, width), 1), 5)
    for h in range(heads):
        high, low = 16 * h, 16 * (heads + h)
        own = feature_head == h
        head_readout[high : high + 16] = jnp.where(own, readout_hi, 0.0).astype(BF16)
        head_readout[low : low + 16] = jnp.where(own, readout_lo, 0.0).astype(BF16)

    index = frag_atoms[...]
    live = jnp.where(index >= 0, 1.0, 0.0)
    active = to_column(jnp.where(assign[0:1, :] >= 0, 1.0, 0.0))
    count = jnp.sum(live, axis=1, keepdims=True) * active
    left_rows = iota((pairs, LANES), 1) < atoms
    counts[...] = jnp.where(left_rows, count[0:pairs], count[pairs:])
    start = jnp.maximum(index[:, 0:1], 0) + HALO
    tile_of = lax.shift_right_logical(start, 7)
    shift = jnp.bitwise_and(start, 127)
    both = jnp.concatenate([tile_of, tile_of + 1], axis=0)
    pick = jnp.where(iota((2 * slots, ext_rows), 1) == both, 1.0, 0.0)
    pick = jnp.concatenate([pick, pick, pick], axis=1).astype(BF16)
    put = jnp.where(
        iota((ext_rows, 2 * slots), 0).astype(F32) == to_row(both.astype(F32)), 1.0, 0.0
    )
    put = jnp.concatenate([put, put], axis=1).astype(BF16)
    half_lane = jnp.bitwise_and(lane, atoms - 1)
    ahead = half_lane + shift
    pick_lane = jnp.bitwise_and(ahead, 127)
    pick_first = ahead < LANES
    second = jnp.where(iota((slots, LANES), 0) < pairs, 0, atoms)
    put_lane = jnp.bitwise_and(lane - shift + second, 127)
    put_first = lane >= shift

    sub8 = iota((8, LANES), 0)
    lane8 = iota((8, LANES), 1)
    lane64 = iota((atoms, LANES), 1)
    sub64 = iota((atoms, LANES), 0)
    left8 = lane8 < atoms
    left16 = iota((16, LANES), 1) < atoms
    left64 = lane64 < atoms
    other = jnp.bitwise_and(lane64, atoms - 1)
    latest = jnp.maximum(sub64, other).astype(F32)
    distinct = sub64 != other
    keep_left = jnp.where(left64, 1.0, 0.0).astype(BF16)
    keep_right = jnp.where(left64, 0.0, 1.0).astype(BF16)
    per_group = LANES // head_width
    groups = heads // per_group
    half_scale = 0.5 / math.sqrt(head_width)
    decay_rows = [
        -jnp.where(left8[0:1], head_decay[:, 2 * t : 2 * t + 1], head_decay[:, 2 * t + 1 : 2 * t + 2])
        for t in range(heads // 2)
    ]
    flat_masks = [
        jnp.where(sub8 == 2 * t + jnp.where(left8, 0, 1), 1.0, 0.0) for t in range(heads // 2)
    ]
    empty = jnp.zeros((head_width, LANES), BF16)

    for copy in copies:
        copy.wait()
    for side, row in ((0, 0), (1, tiles + 1)):
        for c in range(8):
            ext[c, row : row + 1, :] = rim_in[0, side, c : c + 1, :]
    ext[7] = TIME_STEP / ext[7]
    shared = (iota((2, LANES), 0) == 0) == (iota((2, LANES), 1) >= HALO)

    def gather(components):
        field = jnp.concatenate([ext[c] for c in components], axis=1)
        high = field.astype(BF16)
        rest = field - high.astype(F32)
        middle = rest.astype(BF16)
        low = (rest - middle.astype(F32)).astype(BF16)
        picked = dot_nn(pick, jnp.concatenate([high, middle, low], axis=0))
        result = []
        for c in range(len(components)):
            span = slice(c * LANES, (c + 1) * LANES)
            result.append(
                jnp.where(
                    pick_first,
                    lane_pick(picked[0:slots, span], pick_lane),
                    lane_pick(picked[slots:, span], pick_lane),
                )
            )
        return result

    quads = pairs // 2
    many = range(pairs)
    nothing = jnp.zeros((48, LANES), BF16)

    norm_row = jnp.bitwise_and(sub8, 3) == 0
    own_lanes = (sub8 < 4) == left8

    def set_places(centred):
        norm = centred[0] * centred[0] + centred[1] * centred[1] + centred[2] * centred[2]
        for c, values in enumerate([norm] + centred):
            places[:, c, :] = values[0:pairs]
            places[:, c + 4, :] = values[pairs:]

    def distance_factors(pair):
        place = places[pair]
        high = place.astype(BF16).astype(F32)
        middle = (place - high).astype(BF16).astype(F32)
        low = place - high - middle
        high_one = jnp.where(norm_row, 1.0, high)
        left = [high, middle, low, high_one, jnp.where(norm_row, 1.0, middle), high_one]
        once = jnp.where(norm_row, 1.0, -2.0 * high)
        cross = -2.0 * middle
        right = [
            once,
            once,
            once,
            jnp.where(norm_row, high, cross),
            jnp.where(norm_row, middle, cross),
            jnp.where(norm_row, low, -2.0 * low),
        ]
        right = [jnp.where(own_lanes, part, 0.0) for part in right]
        return jnp.concatenate(left, axis=0), jnp.concatenate(right, axis=0).astype(BF16)

    def model():
        far, hidden = [], []
        for u in range(quads):
            left, right = zip(distance_factors(2 * u), distance_factors(2 * u + 1))
            left = jnp.transpose(jnp.concatenate(left, axis=0))[0:atoms].astype(BF16)
            right = jnp.concatenate(
                [
                    jnp.concatenate([right[0], nothing], axis=0),
                    jnp.concatenate([nothing, right[1]], axis=0),
                ],
                axis=1,
            )
            squared = dot_nn(left, right)
            for v in range(2):
                inside = latest < counts[2 * u + v : 2 * u + v + 1, :]
                far.append(jnp.where(inside, squared[:, v * LANES : (v + 1) * LANES], FAR))
        summed = []
        for k in many:
            nearby = jnp.where(distinct, jnp.exp(-NEAR_RATE * far[k]), 0.0)
            near_hi = nearby.astype(BF16)
            near_lo = (nearby - near_hi.astype(F32)).astype(BF16)
            block = jnp.concatenate(
                [
                    jnp.concatenate([near * keep_left, near * keep_right], axis=0)
                    for near in (near_hi, near_lo)
                ],
                axis=1,
            )
            span = slice(k * LANES, (k + 1) * LANES)
            theirs = neigh_rows[span, :]
            summed.append(dot_nn(block, jnp.concatenate([theirs, theirs], axis=0)))
        for k in many:
            span = slice(k * LANES, (k + 1) * LANES)
            hidden.append(silu_of_double(summed[k] + own_rows[span, :]).astype(BF16))
        query, key, value, base, reads = {}, {}, {}, {}, {}
        parts, weights, mixed, lefts = {}, {}, {}, {}

        def project(u):
            block = jnp.concatenate(hidden[2 * u : 2 * u + 2], axis=0)
            query[u] = dot_nn(block, w_query[...]).astype(BF16)
            across = dot_nt(projections[...], block)
            key[u] = across[0:width].astype(BF16)
            value[u] = across[width : 2 * width].astype(BF16)
            base[u] = across[2 * width : 2 * width + 16] + across[2 * width + 16 :]

        def read(u):
            product = dot_nn(head_readout[...], value[u])
            reads[u] = product[0 : 16 * heads] + product[16 * heads :]

        def score(k):
            u, span = k // 2, slice((k % 2) * LANES, (k % 2 + 1) * LANES)
            straight = key[u][:, span]
            turned = pltpu.roll(straight, atoms, 1)
            result = []
            for m in range(2):
                at = (2 * (k % 2) + m) * atoms
                scored = []
                for g in range(groups):
                    blocks = []
                    for h in range(per_group):
                        feature = slice(
                            g * LANES + h * head_width, g * LANES + (h + 1) * head_width
                        )
                        source = straight if h % 2 == m else turned
                        keep = keep_left if h % 2 == 0 else keep_right
                        piece = source[feature] * keep[0:head_width]
                        blocks.append(
                            jnp.concatenate(
                                [piece if t == h // 2 else empty for t in range(per_group // 2)],
                                axis=1,
                            )
                        )
                    scored.append(
                        dot_nn(
                            query[u][at : at + atoms, g * LANES : (g + 1) * LANES],
                            jnp.concatenate(blocks, axis=0),
                        )
                    )
                result.append(scored)
            parts[k] = result

        def weigh(k):
            turned = pltpu.roll(far[k], atoms, 1)
            result = []
            for m in range(2):
                here = jnp.where(left64, far[k], turned) if m == 0 else jnp.where(left64, turned, far[k])
                tiles_out = []
                for t in range(heads // 2):
                    part = parts[k][m][t // 2][:, (t % 2) * LANES : (t % 2 + 1) * LANES]
                    envelope = jnp.exp(here * decay_rows[t])
                    tiles_out.append((silu_of_double(part * half_scale) * envelope).astype(BF16))
                result.append(jnp.concatenate(tiles_out, axis=1))
            weights[k] = jnp.concatenate(result, axis=0)

        def mix(k):
            u, span = k // 2, slice((k % 2) * LANES, (k % 2 + 1) * LANES)
            straight = reads[u][:, span]
            turned = pltpu.roll(straight, atoms, 1)
            left = []
            for m in range(2):
                a, b = (straight, turned) if m == 0 else (turned, straight)
                left.append(
                    jnp.concatenate(
                        [
                            jnp.where(
                                left16,
                                a[32 * t : 32 * t + 16],
                                b[32 * t + 16 : 32 * t + 32],
                            )
                            for t in range(heads // 2)
                        ],
                        axis=1,
                    )
                )
            left = jnp.concatenate(left, axis=0)
            left_hi = left.astype(BF16)
            left_lo = (left - left_hi.astype(F32)).astype(BF16)
            product = dot_nt(jnp.concatenate([left_hi, left_lo], axis=0), weights[k])
            mixed[k] = product[0:32] + product[32:64]

        def flatten(k):
            u, span = k // 2, slice((k % 2) * LANES, (k % 2 + 1) * LANES)
            scalars = jnp.where(left16, mixed[k][0:16], mixed[k][16:32]) + base[u][:, span]
            atom_energy[k : k + 1, :] = scalars[heads : heads + 1]
            straight = scalars[0:heads]
            turned = pltpu.roll(straight, atoms, 1)
            place = places[k]
            swapped = pltpu.roll(place, 4, 0)
            left = []
            for m in range(2):
                a, b = (straight, turned) if m == 0 else (turned, straight)
                here = jnp.where(left8, a, b)
                a, b = (place, swapped) if m == 0 else (swapped, place)
                spot = jnp.where(norm_row, 1.0, jnp.where(sub8 < 4, a, b))
                terms = []
                for t in range(heads // 2):
                    term = jnp.sum(here * flat_masks[t], axis=0, keepdims=True) * spot
                    term_hi = term.astype(BF16).astype(F32)
                    terms.append(jnp.where(sub8 < 4, term_hi, term - term_hi))
                left.append(jnp.concatenate(terms, axis=1))
            lefts[k] = jnp.concatenate(left, axis=0).astype(BF16)

        def pull(k):
            pulled = dot_nt(lefts[k], weights[k])
            pulls[k] = jnp.where(left8, pulled[0:8], pulled[8:16])

        steps = dict(
            project=project, read=read, score=score, weigh=weigh, mix=mix, flatten=flatten, pull=pull
        )
        for name, k in order_of_work(quads):
            steps[name](k)

    def finish_energy(step):
        each = atom_energy[...]
        energy = jnp.concatenate(
            [
                jnp.sum(jnp.where(left_rows, each, 0.0), axis=1, keepdims=True),
                jnp.sum(jnp.where(left_rows, 0.0, each), axis=1, keepdims=True),
            ],
            axis=0,
        )
        energies_out[step : step + 1, :] = to_row(energy)

    def hand_out(which):
        for tile in which:
            span = pl.ds(tile * LANES, LANES)
            for c in range(3):
                positions_out[c : c + 1, span] = ext[c, tile + 1 : tile + 2, :]
                velocities_out[c : c + 1, span] = ext[4 + c, tile + 1 : tile + 2, :]

    for step in range(STEPS):
        fields = gather((0, 1, 2, 3) if step == 0 else (0, 1, 2))
        centred = [field - field[:, 0:1] for field in fields[:3]]
        for c in range(3):
            rows[c] = jnp.where(left_rows, centred[c][0:pairs], centred[c][pairs:])
        set_places(centred)
        if step == 0:
            sort = jnp.where(half_lane.astype(F32) < count, fields[3], -1.0)
            cols[...] = jnp.transpose(jnp.concatenate([sort] * (LANES // slots), axis=0))[0:atoms]
            both_tables = jnp.concatenate([embed[...] * 0.5, neigh[...] * 0.5], axis=1).astype(BF16)

            for u in range(quads):
                hot = []
                for k in (2 * u, 2 * u + 1):
                    for m in range(2):
                        at = jnp.full((atoms, LANES), m * pairs + k, jnp.int32)
                        kind = lane_pick(cols[...], at)
                        hot.append(jnp.where(kind == lane64.astype(F32), 1.0, 0.0))
                hot = jnp.concatenate(hot, axis=0).astype(BF16)[:, 0:types]
                found = dot_nn(hot, both_tables)
                span = slice(2 * u * LANES, (2 * u + 2) * LANES)
                own_rows[span, :] = found[:, 0:width]
                neigh_rows[span, :] = found[:, width:].astype(BF16)
        model()

        sums = [pulls[:, q, :] + pulls[:, q + 4, :] for q in range(4)]
        placed_here, placed_next = [], []
        for c in range(3):
            force = rows[c] * sums[0] - sums[c + 1]
            force = jnp.concatenate(
                [jnp.where(left_rows, force, 0.0), jnp.where(left_rows, 0.0, force)], axis=0
            )
            turned = lane_pick(force, put_lane)
            placed_here.append(jnp.where(put_first, turned, 0.0))
            placed_next.append(jnp.where(put_first, 0.0, turned))
        placed = jnp.concatenate(
            [jnp.concatenate(placed_here, axis=1), jnp.concatenate(placed_next, axis=1)], axis=0
        )
        placed_hi = placed.astype(BF16)
        placed_lo = (placed - placed_hi.astype(F32)).astype(BF16)
        total = dot_nn(put, jnp.concatenate([placed_hi, placed_lo], axis=0))
        total = [total[:, c * LANES : (c + 1) * LANES] for c in range(3)]

        phase = step + 1
        for c in range(3):
            rim_out[phase, 0, 2 * c : 2 * c + 2, :] = total[c][tiles : tiles + 2]
            rim_out[phase, 1, 2 * c : 2 * c + 2, :] = total[c][0:2]
        copies = exchange(phase)
        for c in range(3):
            moved = ext[4 + c] + total[c] * ext[7]
            ext[4 + c] = moved
            ext[c] = ext[c] + TIME_STEP * moved
        finish_energy(step)
        if step == STEPS - 1:
            hand_out(range(1, tiles - 1))
        for copy in copies:
            copy.wait()
        for side, row in ((0, 0), (1, tiles)):
            border = slice(row, row + 2)
            for c in range(3):
                extra = jnp.where(shared, rim_in[phase, side, 2 * c : 2 * c + 2, :], 0.0)
                kick = extra * ext[7, border, :]
                ext[4 + c, border, :] = ext[4 + c, border, :] + kick
                ext[c, border, :] = ext[c, border, :] + TIME_STEP * kick
    hand_out((0, tiles - 1))


def hand_over(*refs):
    for k in range(3):
        refs[k + 3][...] = refs[k][...]


def body(
    positions,
    velocities,
    masses,
    atom_kinds,
    frag_atoms,
    assign,
    embed_table,
    neigh_table,
    w_query,
    w_key,
    w_value,
    w_energy,
    w_force,
    head_decay,
):
    tiles = positions.shape[1] // LANES
    slots, atoms = frag_atoms.shape
    heads = head_decay.shape[0]
    width = w_query.shape[0]
    ext_rows = -(-(tiles + 3) // 8) * 8
    vmem = pl.BlockSpec(memory_space=pltpu.VMEM)
    operands = (
        positions,
        velocities,
        masses.reshape(tiles, LANES),
        atom_kinds.reshape(tiles, LANES),
        frag_atoms,
        assign,
        embed_table,
        neigh_table,
        w_query,
        w_key,
        w_value,
        w_energy.reshape(1, width),
        w_force.T,
        head_decay.reshape(1, heads),
    )
    results = pl.pallas_call(
        functools.partial(kernel, tiles, slots, heads),
        out_shape=(
            jax.ShapeDtypeStruct(positions.shape, F32),
            jax.ShapeDtypeStruct(velocities.shape, F32),
            jax.ShapeDtypeStruct((STEPS, slots), F32),
        ),
        in_specs=[pl.BlockSpec(memory_space=pltpu.HBM)] * OPERANDS,
        out_specs=(vmem, vmem, vmem),
        scratch_shapes=[pltpu.VMEM(operand.shape, operand.dtype) for operand in operands]
        + [
            pltpu.VMEM((8, ext_rows, LANES), F32),
            pltpu.VMEM((STEPS + 1, 2, 8, LANES), F32),
            pltpu.VMEM((STEPS + 1, 2, 8, LANES), F32),
            pltpu.VMEM((3, slots // 2, LANES), F32),
            pltpu.VMEM((atoms, LANES), F32),
            pltpu.VMEM((slots // 2, LANES), F32),
            pltpu.VMEM((slots // 2, 8, LANES), F32),
            pltpu.VMEM((slots * atoms, width), F32),
            pltpu.VMEM((slots * atoms, width), BF16),
            pltpu.VMEM((2 * width + 32, width), BF16),
            pltpu.VMEM((32 * heads, width), BF16),
            pltpu.VMEM((slots // 2, 8, LANES), F32),
            pltpu.VMEM((slots // 2, LANES), F32),
            pltpu.SemaphoreType.DMA((OPERANDS,)),
            pltpu.SemaphoreType.DMA((STEPS + 1, 2)),
            pltpu.SemaphoreType.DMA((STEPS + 1, 2)),
        ],
        compiler_params=pltpu.CompilerParams(
            collective_id=0, has_side_effects=True, vmem_limit_bytes=56 * 1024 * 1024
        ),
    )(*operands)
    return pl.pallas_call(
        hand_over,
        out_shape=tuple(jax.ShapeDtypeStruct(result.shape, F32) for result in results),
        in_specs=[vmem] * 3,
        out_specs=(vmem,) * 3,
        compiler_params=pltpu.CompilerParams(vmem_limit_bytes=56 * 1024 * 1024),
    )(*results)


def solution(mesh):
    both = ("dom", "grp")
    return jax.shard_map(
        body,
        mesh=mesh,
        in_specs=(
            P(None, both),
            P(None, both),
            P(both),
            P(both),
            P(both, None),
            P(None, both),
        )
        + (P(),) * 8,
        out_specs=(P(None, both), P(None, both), P(None, both)),
        check_vma=False,
    )
```

```python
import functools
import math

import jax
import jax.numpy as jnp
from jax import lax
from jax.experimental import pallas as pl
from jax.experimental.pallas import tpu as pltpu
from jax.sharding import PartitionSpec as P

HALO = 64
STEPS = 2
TIME_STEP = 0.05
NEAR_RATE = 0.5
FAR = 1e30
LANES = 128
OPERANDS = 14
F32 = jnp.float32
BF16 = jnp.bfloat16


def dot_nn(a, b):
    return lax.dot_general(a, b, (((1,), (0,)), ((), ())), preferred_element_type=F32)


def dot_nt(a, b):
    return lax.dot_general(a, b, (((1,), (1,)), ((), ())), preferred_element_type=F32)


def lane_pick(x, index):
    return jnp.take_along_axis(x, index, axis=1, mode="promise_in_bounds")


def iota(shape, dim):
    return lax.broadcasted_iota(jnp.int32, shape, dim)


def to_row(column):
    size = column.shape[0]
    same = iota((size, size), 0) == iota((size, size), 1)
    return jnp.sum(jnp.where(same, column, 0.0), axis=0, keepdims=True)


def to_column(row):
    size = row.shape[1]
    same = iota((size, size), 0) == iota((size, size), 1)
    return jnp.sum(jnp.where(same, row, 0.0), axis=1, keepdims=True)


def silu_of_double(half):
    return half + half * jnp.tanh(half)


def order_of_work(quads):
    many = range(2 * quads)
    order = [("project", u) for u in range(quads)] + [("read", u) for u in range(quads)]
    order.append(("score", 0))
    for k in many:
        if k + 1 in many:
            order.append(("score", k + 1))
        order.append(("weigh", k))
        if k - 2 in many:
            order.append(("mix", k - 2))
        if k - 4 in many:
            order.append(("flatten", k - 4))
        if k - 6 in many:
            order.append(("pull", k - 6))
    order += [("mix", k) for k in many[-2:]]
    order += [("flatten", k) for k in many[-4:]]
    order += [("pull", k) for k in many[-6:]]
    return order


def kernel(tiles, slots, heads, *refs):
    doms = lax.axis_size("dom")
    me = lax.axis_index("dom")
    upper, lower = lax.rem(me + 1, doms), lax.rem(me + doms - 1, doms)
    barrier = pltpu.get_barrier_semaphore()
    for neighbour in (lower, upper):
        pl.semaphore_signal(
            barrier, inc=1, device_id={"dom": neighbour}, device_id_type=pl.DeviceIdType.MESH
        )

    operands, refs = refs[:OPERANDS], refs[OPERANDS:]
    (positions_out, velocities_out, energies_out), refs = refs[:3], refs[3:]
    local, refs = refs[:OPERANDS], refs[OPERANDS:]
    (
        ext,
        rim_out,
        rim_in,
        rows,
        cols,
        counts,
        places,
        own_rows,
        neigh_rows,
        projections,
        head_readout,
        pulls,
        atom_energy,
        load_sem,
        send_sem,
        recv_sem,
    ) = refs
    loads = [
        pltpu.make_async_copy(source, target, load_sem.at[k])
        for k, (source, target) in enumerate(zip(operands, local))
    ]
    for load in loads:
        load.start()
    (
        positions,
        velocities,
        masses,
        kinds,
        frag_atoms,
        assign,
        embed,
        neigh,
        w_query,
        w_key,
        w_value,
        w_energy,
        w_force,
        head_decay,
    ) = local
    width = w_query.shape[0]
    head_width = width // heads
    ext_rows = ext.shape[1]
    types = embed.shape[0]

    lane = iota((slots, LANES), 1)

    for load in loads[:4]:
        load.wait()
    for side, tile in ((0, tiles - 1), (1, 0)):
        span = pl.ds(tile * LANES, LANES)
        rim_out[0, side, 0:3, :] = positions[:, span]
        rim_out[0, side, 3:4, :] = kinds[tile : tile + 1, :].astype(F32)
        rim_out[0, side, 4:7, :] = velocities[:, span]
        rim_out[0, side, 7:8, :] = masses[tile : tile + 1, :]

    def exchange(phase):
        copies = []
        for side, target in ((0, upper), (1, lower)):
            copy = pltpu.make_async_remote_copy(
                src_ref=rim_out.at[phase, side],
                dst_ref=rim_in.at[phase, side],
                send_sem=send_sem.at[phase, side],
                recv_sem=recv_sem.at[phase, side],
                device_id={"dom": target},
                device_id_type=pl.DeviceIdType.MESH,
            )
            copy.start()
            copies.append(copy)
        return copies

    pl.semaphore_wait(barrier, 2)
    copies = exchange(0)

    for tile in range(tiles):
        span = pl.ds(tile * LANES, LANES)
        for c in range(3):
            ext[c, tile + 1 : tile + 2, :] = positions[c : c + 1, span]
            ext[4 + c, tile + 1 : tile + 2, :] = velocities[c : c + 1, span]
    ext[3, 1 : tiles + 1, :] = kinds[...].astype(F32)
    ext[7, 1 : tiles + 1, :] = masses[...]
    for c in range(8):
        ext[c, tiles + 2 : ext_rows, :] = jnp.full((ext_rows - tiles - 2, LANES), 1.0, F32)
    for phase in range(1, STEPS + 1):
        for side in range(2):
            rim_out[phase, side, 6:8, :] = jnp.zeros((2, LANES), F32)

    for load in loads[4:]:
        load.wait()
    readout = jnp.concatenate(
        [
            w_force[...],
            w_energy[...],
            jnp.zeros((15 - heads, width), F32),
        ],
        axis=0,
    )
    readout_hi = readout.astype(BF16).astype(F32)
    readout_lo = readout - readout_hi
    atoms = frag_atoms.shape[1]
    pairs = slots // 2
    projections[0:width] = jnp.transpose(w_key[...].astype(F32)).astype(BF16)
    projections[width : 2 * width] = jnp.transpose(w_value[...].astype(F32)).astype(BF16)
    projections[2 * width : 2 * width + 16] = readout_hi.astype(BF16)
    projections[2 * width + 16 : 2 * width + 32] = readout_lo.astype(BF16)
    feature_head = lax.shift_right_logical(iota((16, width), 1), 5)
    for h in range(heads):
        high, low = 16 * h, 16 * (heads + h)
        own = feature_head == h
        head_readout[high : high + 16] = jnp.where(own, readout_hi, 0.0).astype(BF16)
        head_readout[low : low + 16] = jnp.where(own, readout_lo, 0.0).astype(BF16)

    index = frag_atoms[...]
    live = jnp.where(index >= 0, 1.0, 0.0)
    active = to_column(jnp.where(assign[0:1, :] >= 0, 1.0, 0.0))
    count = jnp.sum(live, axis=1, keepdims=True) * active
    left_rows = iota((pairs, LANES), 1) < atoms
    counts[...] = jnp.where(left_rows, count[0:pairs], count[pairs:])
    start = jnp.maximum(index[:, 0:1], 0) + HALO
    tile_of = lax.shift_right_logical(start, 7)
    shift = jnp.bitwise_and(start, 127)
    both = jnp.concatenate([tile_of, tile_of + 1], axis=0)
    pick = jnp.where(iota((2 * slots, ext_rows), 1) == both, 1.0, 0.0)
    pick = jnp.concatenate([pick, pick, pick], axis=1).astype(BF16)
    put = jnp.where(
        iota((ext_rows, 2 * slots), 0).astype(F32) == to_row(both.astype(F32)), 1.0, 0.0
    )
    put = jnp.concatenate([put, put], axis=1).astype(BF16)
    half_lane = jnp.bitwise_and(lane, atoms - 1)
    ahead = half_lane + shift
    pick_lane = jnp.bitwise_and(ahead, 127)
    pick_first = ahead < LANES
    second = jnp.where(iota((slots, LANES), 0) < pairs, 0, atoms)
    put_lane = jnp.bitwise_and(lane - shift + second, 127)
    put_first = lane >= shift

    sub8 = iota((8, LANES), 0)
    lane8 = iota((8, LANES), 1)
    lane64 = iota((atoms, LANES), 1)
    sub64 = iota((atoms, LANES), 0)
    left8 = lane8 < atoms
    left16 = iota((16, LANES), 1) < atoms
    left64 = lane64 < atoms
    other = jnp.bitwise_and(lane64, atoms - 1)
    latest = jnp.maximum(sub64, other).astype(F32)
    distinct = sub64 != other
    keep_left = jnp.where(left64, 1.0, 0.0).astype(BF16)
    keep_right = jnp.where(left64, 0.0, 1.0).astype(BF16)
    per_group = LANES // head_width
    groups = heads // per_group
    half_scale = 0.5 / math.sqrt(head_width)
    decay_rows = [
        -jnp.where(left8[0:1], head_decay[:, 2 * t : 2 * t + 1], head_decay[:, 2 * t + 1 : 2 * t + 2])
        for t in range(heads // 2)
    ]
    empty = jnp.zeros((head_width, LANES), BF16)

    for copy in copies:
        copy.wait()
    for side, row in ((0, 0), (1, tiles + 1)):
        for c in range(8):
            ext[c, row : row + 1, :] = rim_in[0, side, c : c + 1, :]
    ext[7] = TIME_STEP / ext[7]
    shared = (iota((2, LANES), 0) == 0) == (iota((2, LANES), 1) >= HALO)

    def gather(components):
        field = jnp.concatenate([ext[c] for c in components], axis=1)
        high = field.astype(BF16)
        rest = field - high.astype(F32)
        middle = rest.astype(BF16)
        low = (rest - middle.astype(F32)).astype(BF16)
        picked = dot_nn(pick, jnp.concatenate([high, middle, low], axis=0))
        result = []
        for c in range(len(components)):
            span = slice(c * LANES, (c + 1) * LANES)
            result.append(
                jnp.where(
                    pick_first,
                    lane_pick(picked[0:slots, span], pick_lane),
                    lane_pick(picked[slots:, span], pick_lane),
                )
            )
        return result

    quads = pairs // 2
    many = range(pairs)
    nothing = jnp.zeros((48, LANES), BF16)

    norm_row = jnp.bitwise_and(sub8, 3) == 0
    own_lanes = (sub8 < 4) == left8

    def set_places(centred):
        norm = centred[0] * centred[0] + centred[1] * centred[1] + centred[2] * centred[2]
        for c, values in enumerate([norm] + centred):
            places[:, c, :] = values[0:pairs]
            places[:, c + 4, :] = values[pairs:]

    def distance_factors(pair):
        place = places[pair]
        high = place.astype(BF16).astype(F32)
        middle = (place - high).astype(BF16).astype(F32)
        low = place - high - middle
        high_one = jnp.where(norm_row, 1.0, high)
        left = [high, middle, low, high_one, jnp.where(norm_row, 1.0, middle), high_one]
        once = jnp.where(norm_row, 1.0, -2.0 * high)
        cross = -2.0 * middle
        right = [
            once,
            once,
            once,
            jnp.where(norm_row, high, cross),
            jnp.where(norm_row, middle, cross),
            jnp.where(norm_row, low, -2.0 * low),
        ]
        right = [jnp.where(own_lanes, part, 0.0) for part in right]
        return jnp.concatenate(left, axis=0), jnp.concatenate(right, axis=0).astype(BF16)

    def model():
        far, hidden = [], []
        for u in range(quads):
            left, right = zip(distance_factors(2 * u), distance_factors(2 * u + 1))
            left = jnp.transpose(jnp.concatenate(left, axis=0))[0:atoms].astype(BF16)
            right = jnp.concatenate(
                [
                    jnp.concatenate([right[0], nothing], axis=0),
                    jnp.concatenate([nothing, right[1]], axis=0),
                ],
                axis=1,
            )
            squared = dot_nn(left, right)
            for v in range(2):
                inside = latest < counts[2 * u + v : 2 * u + v + 1, :]
                far.append(jnp.where(inside, squared[:, v * LANES : (v + 1) * LANES], FAR))
        summed = []
        for k in many:
            nearby = jnp.where(distinct, jnp.exp(-NEAR_RATE * far[k]), 0.0)
            near_hi = nearby.astype(BF16)
            near_lo = (nearby - near_hi.astype(F32)).astype(BF16)
            block = jnp.concatenate(
                [
                    jnp.concatenate([near * keep_left, near * keep_right], axis=0)
                    for near in (near_hi, near_lo)
                ],
                axis=1,
            )
            span = slice(k * LANES, (k + 1) * LANES)
            theirs = neigh_rows[span, :]
            summed.append(dot_nn(block, jnp.concatenate([theirs, theirs], axis=0)))
        for k in many:
            span = slice(k * LANES, (k + 1) * LANES)
            hidden.append(silu_of_double(summed[k] + own_rows[span, :]).astype(BF16))
        query, key, value, base, reads = {}, {}, {}, {}, {}
        parts, weights, mixed, lefts = {}, {}, {}, {}

        def project(u):
            block = jnp.concatenate(hidden[2 * u : 2 * u + 2], axis=0)
            query[u] = dot_nn(block, w_query[...]).astype(BF16)
            across = dot_nt(projections[...], block)
            key[u] = across[0:width].astype(BF16)
            value[u] = across[width : 2 * width].astype(BF16)
            base[u] = across[2 * width : 2 * width + 16] + across[2 * width + 16 :]

        def read(u):
            product = dot_nn(head_readout[...], value[u])
            reads[u] = product[0 : 16 * heads] + product[16 * heads :]

        def score(k):
            u, span = k // 2, slice((k % 2) * LANES, (k % 2 + 1) * LANES)
            straight = key[u][:, span]
            turned = pltpu.roll(straight, atoms, 1)
            result = []
            for m in range(2):
                at = (2 * (k % 2) + m) * atoms
                scored = []
                for g in range(groups):
                    blocks = []
                    for h in range(per_group):
                        feature = slice(
                            g * LANES + h * head_width, g * LANES + (h + 1) * head_width
                        )
                        source = straight if h % 2 == m else turned
                        keep = keep_left if h % 2 == 0 else keep_right
                        piece = source[feature] * keep[0:head_width]
                        blocks.append(
                            jnp.concatenate(
                                [piece if t == h // 2 else empty for t in range(per_group // 2)],
                                axis=1,
                            )
                        )
                    scored.append(
                        dot_nn(
                            query[u][at : at + atoms, g * LANES : (g + 1) * LANES],
                            jnp.concatenate(blocks, axis=0),
                        )
                    )
                result.append(scored)
            parts[k] = result

        def weigh(k):
            turned = pltpu.roll(far[k], atoms, 1)
            result = []
            for m in range(2):
                here = jnp.where(left64, far[k], turned) if m == 0 else jnp.where(left64, turned, far[k])
                tiles_out = []
                for t in range(heads // 2):
                    part = parts[k][m][t // 2][:, (t % 2) * LANES : (t % 2 + 1) * LANES]
                    envelope = jnp.exp(here * decay_rows[t])
                    tiles_out.append((silu_of_double(part * half_scale) * envelope).astype(BF16))
                result.append(jnp.concatenate(tiles_out, axis=1))
            weights[k] = jnp.concatenate(result, axis=0)

        def mix(k):
            u, span = k // 2, slice((k % 2) * LANES, (k % 2 + 1) * LANES)
            straight = reads[u][:, span]
            turned = pltpu.roll(straight, atoms, 1)
            left = []
            for m in range(2):
                a, b = (straight, turned) if m == 0 else (turned, straight)
                left.append(
                    jnp.concatenate(
                        [
                            jnp.where(
                                left16,
                                a[32 * t : 32 * t + 16],
                                b[32 * t + 16 : 32 * t + 32],
                            )
                            for t in range(heads // 2)
                        ],
                        axis=1,
                    )
                )
            left = jnp.concatenate(left, axis=0)
            left_hi = left.astype(BF16)
            left_lo = (left - left_hi.astype(F32)).astype(BF16)
            product = dot_nt(jnp.concatenate([left_hi, left_lo], axis=0), weights[k])
            mixed[k] = product[0:32] + product[32:64]

        def flatten(k):
            u, span = k // 2, slice((k % 2) * LANES, (k % 2 + 1) * LANES)
            scalars = jnp.where(left16, mixed[k][0:16], mixed[k][16:32]) + base[u][:, span]
            atom_energy[k : k + 1, :] = scalars[heads : heads + 1]
            straight = scalars[0:heads]
            turned = pltpu.roll(straight, atoms, 1)
            place = places[k]
            swapped = pltpu.roll(place, 4, 0)
            left = []
            for m in range(2):
                low, high = (straight, turned) if m == 0 else (turned, straight)
                a, b = (place, swapped) if m == 0 else (swapped, place)
                spot = jnp.where(norm_row, 1.0, jnp.where(sub8 < 4, a, b))
                terms = []
                for t in range(heads // 2):
                    flat = jnp.where(left8, low[2 * t : 2 * t + 1], high[2 * t + 1 : 2 * t + 2])
                    term = flat * spot
                    term_hi = term.astype(BF16).astype(F32)
                    terms.append(jnp.where(sub8 < 4, term_hi, term - term_hi))
                left.append(jnp.concatenate(terms, axis=1))
            lefts[k] = jnp.concatenate(left, axis=0).astype(BF16)

        def pull(k):
            pulled = dot_nt(lefts[k], weights[k])
            pulls[k] = jnp.where(left8, pulled[0:8], pulled[8:16])

        steps = dict(
            project=project, read=read, score=score, weigh=weigh, mix=mix, flatten=flatten, pull=pull
        )
        for name, k in order_of_work(quads):
            steps[name](k)

    def finish_energy(step):
        each = atom_energy[...]
        energy = jnp.concatenate(
            [
                jnp.sum(jnp.where(left_rows, each, 0.0), axis=1, keepdims=True),
                jnp.sum(jnp.where(left_rows, 0.0, each), axis=1, keepdims=True),
            ],
            axis=0,
        )
        energies_out[step : step + 1, :] = to_row(energy)

    def hand_out(which):
        for tile in which:
            span = pl.ds(tile * LANES, LANES)
            for c in range(3):
                positions_out[c : c + 1, span] = ext[c, tile + 1 : tile + 2, :]
                velocities_out[c : c + 1, span] = ext[4 + c, tile + 1 : tile + 2, :]

    for step in range(STEPS):
        fields = gather((0, 1, 2, 3) if step == 0 else (0, 1, 2))
        centred = [field - field[:, 0:1] for field in fields[:3]]
        for c in range(3):
            rows[c] = jnp.where(left_rows, centred[c][0:pairs], centred[c][pairs:])
        set_places(centred)
        if step == 0:
            sort = jnp.where(half_lane.astype(F32) < count, fields[3], -1.0)
            cols[...] = jnp.transpose(jnp.concatenate([sort] * (LANES // slots), axis=0))[0:atoms]
            both_tables = jnp.concatenate([embed[...] * 0.5, neigh[...] * 0.5], axis=1).astype(BF16)

            for u in range(quads):
                hot = []
                for k in (2 * u, 2 * u + 1):
                    for m in range(2):
                        at = jnp.full((atoms, LANES), m * pairs + k, jnp.int32)
                        kind = lane_pick(cols[...], at)
                        hot.append(jnp.where(kind == lane64.astype(F32), 1.0, 0.0))
                hot = jnp.concatenate(hot, axis=0).astype(BF16)[:, 0:types]
                found = dot_nn(hot, both_tables)
                span = slice(2 * u * LANES, (2 * u + 2) * LANES)
                own_rows[span, :] = found[:, 0:width]
                neigh_rows[span, :] = found[:, width:].astype(BF16)
        model()

        sums = [pulls[:, q, :] + pulls[:, q + 4, :] for q in range(4)]
        placed_here, placed_next = [], []
        for c in range(3):
            force = rows[c] * sums[0] - sums[c + 1]
            force = jnp.concatenate(
                [jnp.where(left_rows, force, 0.0), jnp.where(left_rows, 0.0, force)], axis=0
            )
            turned = lane_pick(force, put_lane)
            placed_here.append(jnp.where(put_first, turned, 0.0))
            placed_next.append(jnp.where(put_first, 0.0, turned))
        placed = jnp.concatenate(
            [jnp.concatenate(placed_here, axis=1), jnp.concatenate(placed_next, axis=1)], axis=0
        )
        placed_hi = placed.astype(BF16)
        placed_lo = (placed - placed_hi.astype(F32)).astype(BF16)
        total = dot_nn(put, jnp.concatenate([placed_hi, placed_lo], axis=0))
        total = [total[:, c * LANES : (c + 1) * LANES] for c in range(3)]

        phase = step + 1
        for c in range(3):
            rim_out[phase, 0, 2 * c : 2 * c + 2, :] = total[c][tiles : tiles + 2]
            rim_out[phase, 1, 2 * c : 2 * c + 2, :] = total[c][0:2]
        copies = exchange(phase)
        for c in range(3):
            moved = ext[4 + c] + total[c] * ext[7]
            ext[4 + c] = moved
            ext[c] = ext[c] + TIME_STEP * moved
        finish_energy(step)
        if step == STEPS - 1:
            hand_out(range(1, tiles - 1))
        for copy in copies:
            copy.wait()
        for side, row in ((0, 0), (1, tiles)):
            border = slice(row, row + 2)
            for c in range(3):
                extra = jnp.where(shared, rim_in[phase, side, 2 * c : 2 * c + 2, :], 0.0)
                kick = extra * ext[7, border, :]
                ext[4 + c, border, :] = ext[4 + c, border, :] + kick
                ext[c, border, :] = ext[c, border, :] + TIME_STEP * kick
    hand_out((0, tiles - 1))


def hand_over(*refs):
    for k in range(3):
        refs[k + 3][...] = refs[k][...]


def body(
    positions,
    velocities,
    masses,
    atom_kinds,
    frag_atoms,
    assign,
    embed_table,
    neigh_table,
    w_query,
    w_key,
    w_value,
    w_energy,
    w_force,
    head_decay,
):
    tiles = positions.shape[1] // LANES
    slots, atoms = frag_atoms.shape
    heads = head_decay.shape[0]
    width = w_query.shape[0]
    ext_rows = -(-(tiles + 3) // 8) * 8
    vmem = pl.BlockSpec(memory_space=pltpu.VMEM)
    operands = (
        positions,
        velocities,
        masses.reshape(tiles, LANES),
        atom_kinds.reshape(tiles, LANES),
        frag_atoms,
        assign,
        embed_table,
        neigh_table,
        w_query,
        w_key,
        w_value,
        w_energy.reshape(1, width),
        w_force.T,
        head_decay.reshape(1, heads),
    )
    results = pl.pallas_call(
        functools.partial(kernel, tiles, slots, heads),
        out_shape=(
            jax.ShapeDtypeStruct(positions.shape, F32),
            jax.ShapeDtypeStruct(velocities.shape, F32),
            jax.ShapeDtypeStruct((STEPS, slots), F32),
        ),
        in_specs=[pl.BlockSpec(memory_space=pltpu.HBM)] * OPERANDS,
        out_specs=(vmem, vmem, vmem),
        scratch_shapes=[pltpu.VMEM(operand.shape, operand.dtype) for operand in operands]
        + [
            pltpu.VMEM((8, ext_rows, LANES), F32),
            pltpu.VMEM((STEPS + 1, 2, 8, LANES), F32),
            pltpu.VMEM((STEPS + 1, 2, 8, LANES), F32),
            pltpu.VMEM((3, slots // 2, LANES), F32),
            pltpu.VMEM((atoms, LANES), F32),
            pltpu.VMEM((slots // 2, LANES), F32),
            pltpu.VMEM((slots // 2, 8, LANES), F32),
            pltpu.VMEM((slots * atoms, width), F32),
            pltpu.VMEM((slots * atoms, width), BF16),
            pltpu.VMEM((2 * width + 32, width), BF16),
            pltpu.VMEM((32 * heads, width), BF16),
            pltpu.VMEM((slots // 2, 8, LANES), F32),
            pltpu.VMEM((slots // 2, LANES), F32),
            pltpu.SemaphoreType.DMA((OPERANDS,)),
            pltpu.SemaphoreType.DMA((STEPS + 1, 2)),
            pltpu.SemaphoreType.DMA((STEPS + 1, 2)),
        ],
        compiler_params=pltpu.CompilerParams(
            collective_id=0, has_side_effects=True, vmem_limit_bytes=56 * 1024 * 1024
        ),
    )(*operands)
    return pl.pallas_call(
        hand_over,
        out_shape=tuple(jax.ShapeDtypeStruct(result.shape, F32) for result in results),
        in_specs=[vmem] * 3,
        out_specs=(vmem,) * 3,
        compiler_params=pltpu.CompilerParams(vmem_limit_bytes=56 * 1024 * 1024),
    )(*results)


def solution(mesh):
    both = ("dom", "grp")
    return jax.shard_map(
        body,
        mesh=mesh,
        in_specs=(
            P(None, both),
            P(None, both),
            P(both),
            P(both),
            P(both, None),
            P(None, both),
        )
        + (P(),) * 8,
        out_specs=(P(None, both), P(None, both), P(None, both)),
        check_vma=False,
    )
```

```python
import functools
import math

import jax
import jax.numpy as jnp
from jax import lax
from jax.experimental import pallas as pl
from jax.experimental.pallas import tpu as pltpu
from jax.sharding import PartitionSpec as P

HALO = 64
STEPS = 2
TIME_STEP = 0.05
NEAR_RATE = 0.5
FAR = 1e30
LANES = 128
OPERANDS = 14
F32 = jnp.float32
BF16 = jnp.bfloat16


def dot_nn(a, b):
    return lax.dot_general(a, b, (((1,), (0,)), ((), ())), preferred_element_type=F32)


def dot_nt(a, b):
    return lax.dot_general(a, b, (((1,), (1,)), ((), ())), preferred_element_type=F32)


def lane_pick(x, index):
    return jnp.take_along_axis(x, index, axis=1, mode="promise_in_bounds")


def iota(shape, dim):
    return lax.broadcasted_iota(jnp.int32, shape, dim)


def to_row(column):
    size = column.shape[0]
    same = iota((size, size), 0) == iota((size, size), 1)
    return jnp.sum(jnp.where(same, column, 0.0), axis=0, keepdims=True)


def to_column(row):
    size = row.shape[1]
    same = iota((size, size), 0) == iota((size, size), 1)
    return jnp.sum(jnp.where(same, row, 0.0), axis=1, keepdims=True)


def silu_of_double(half):
    return half + half * jnp.tanh(half)


def order_of_work(quads):
    many = range(2 * quads)
    order = [("project", u) for u in range(quads)] + [("read", u) for u in range(quads)]
    order.append(("score", 0))
    for k in many:
        if k + 1 in many:
            order.append(("score", k + 1))
        order.append(("weigh", k))
        if k - 2 in many:
            order.append(("mix", k - 2))
        if k - 4 in many:
            order.append(("flatten", k - 4))
        if k - 6 in many:
            order.append(("pull", k - 6))
    order += [("mix", k) for k in many[-2:]]
    order += [("flatten", k) for k in many[-4:]]
    order += [("pull", k) for k in many[-6:]]
    return order


def kernel(tiles, slots, heads, *refs):
    doms = lax.axis_size("dom")
    me = lax.axis_index("dom")
    upper, lower = lax.rem(me + 1, doms), lax.rem(me + doms - 1, doms)
    barrier = pltpu.get_barrier_semaphore()
    for neighbour in (lower, upper):
        pl.semaphore_signal(
            barrier, inc=1, device_id={"dom": neighbour}, device_id_type=pl.DeviceIdType.MESH
        )

    operands, refs = refs[:OPERANDS], refs[OPERANDS:]
    (positions_out, velocities_out, energies_out), refs = refs[:3], refs[3:]
    local, refs = refs[:OPERANDS], refs[OPERANDS:]
    (
        ext,
        rim_out,
        rim_in,
        rows,
        cols,
        counts,
        places,
        own_rows,
        neigh_rows,
        projections,
        head_readout,
        pulls,
        atom_energy,
        load_sem,
        send_sem,
        recv_sem,
    ) = refs
    loads = [
        pltpu.make_async_copy(source, target, load_sem.at[k])
        for k, (source, target) in enumerate(zip(operands, local))
    ]
    for load in loads:
        load.start()
    (
        positions,
        velocities,
        masses,
        kinds,
        frag_atoms,
        assign,
        embed,
        neigh,
        w_query,
        w_key,
        w_value,
        w_energy,
        w_force,
        head_decay,
    ) = local
    width = w_query.shape[0]
    head_width = width // heads
    ext_rows = ext.shape[1]
    types = embed.shape[0]

    lane = iota((slots, LANES), 1)

    for load in loads[:4]:
        load.wait()
    for side, tile in ((0, tiles - 1), (1, 0)):
        span = pl.ds(tile * LANES, LANES)
        rim_out[0, side, 0:3, :] = positions[:, span]
        rim_out[0, side, 3:4, :] = kinds[tile : tile + 1, :].astype(F32)
        rim_out[0, side, 4:7, :] = velocities[:, span]
        rim_out[0, side, 7:8, :] = masses[tile : tile + 1, :]

    def exchange(phase):
        copies = []
        for side, target in ((0, upper), (1, lower)):
            copy = pltpu.make_async_remote_copy(
                src_ref=rim_out.at[phase, side],
                dst_ref=rim_in.at[phase, side],
                send_sem=send_sem.at[phase, side],
                recv_sem=recv_sem.at[phase, side],
                device_id={"dom": target},
                device_id_type=pl.DeviceIdType.MESH,
            )
            copy.start()
            copies.append(copy)
        return copies

    pl.semaphore_wait(barrier, 2)
    copies = exchange(0)

    for tile in range(tiles):
        span = pl.ds(tile * LANES, LANES)
        for c in range(3):
            ext[c, tile + 1 : tile + 2, :] = positions[c : c + 1, span]
            ext[4 + c, tile + 1 : tile + 2, :] = velocities[c : c + 1, span]
    ext[3, 1 : tiles + 1, :] = kinds[...].astype(F32)
    ext[7, 1 : tiles + 1, :] = masses[...]
    for c in range(8):
        ext[c, tiles + 2 : ext_rows, :] = jnp.full((ext_rows - tiles - 2, LANES), 1.0, F32)
    for phase in range(1, STEPS + 1):
        for side in range(2):
            rim_out[phase, side, 6:8, :] = jnp.zeros((2, LANES), F32)

    for load in loads[4:]:
        load.wait()
    readout = jnp.concatenate(
        [
            w_force[...],
            w_energy[...],
            jnp.zeros((15 - heads, width), F32),
        ],
        axis=0,
    )
    readout_hi = readout.astype(BF16).astype(F32)
    readout_lo = readout - readout_hi
    atoms = frag_atoms.shape[1]
    pairs = slots // 2
    projections[0:width] = jnp.transpose(w_key[...].astype(F32)).astype(BF16)
    projections[width : 2 * width] = jnp.transpose(w_value[...].astype(F32)).astype(BF16)
    projections[2 * width : 2 * width + 16] = readout_hi.astype(BF16)
    projections[2 * width + 16 : 2 * width + 32] = readout_lo.astype(BF16)
    feature_head = lax.shift_right_logical(iota((16, width), 1), 5)
    for h in range(heads):
        high, low = 16 * h, 16 * (heads + h)
        own = feature_head == h
        head_readout[high : high + 16] = jnp.where(own, readout_hi, 0.0).astype(BF16)
        head_readout[low : low + 16] = jnp.where(own, readout_lo, 0.0).astype(BF16)

    index = frag_atoms[...]
    live = jnp.where(index >= 0, 1.0, 0.0)
    active = to_column(jnp.where(assign[0:1, :] >= 0, 1.0, 0.0))
    count = jnp.sum(live, axis=1, keepdims=True) * active
    left_rows = iota((pairs, LANES), 1) < atoms
    counts[...] = jnp.where(left_rows, count[0:pairs], count[pairs:])
    start = jnp.maximum(index[:, 0:1], 0) + HALO
    tile_of = lax.shift_right_logical(start, 7)
    shift = jnp.bitwise_and(start, 127)
    both = jnp.concatenate([tile_of, tile_of + 1], axis=0)
    pick = jnp.where(iota((2 * slots, ext_rows), 1) == both, 1.0, 0.0)
    pick = jnp.concatenate([pick, pick, pick], axis=1).astype(BF16)
    put = jnp.where(
        iota((ext_rows, 2 * slots), 0).astype(F32) == to_row(both.astype(F32)), 1.0, 0.0
    )
    put = jnp.concatenate([put, put], axis=1).astype(BF16)
    half_lane = jnp.bitwise_and(lane, atoms - 1)
    ahead = half_lane + shift
    pick_lane = jnp.bitwise_and(ahead, 127)
    pick_first = ahead < LANES
    second = jnp.where(iota((slots, LANES), 0) < pairs, 0, atoms)
    put_lane = jnp.bitwise_and(lane - shift + second, 127)
    put_first = lane >= shift

    sub8 = iota((8, LANES), 0)
    lane8 = iota((8, LANES), 1)
    lane64 = iota((atoms, LANES), 1)
    sub64 = iota((atoms, LANES), 0)
    left8 = lane8 < atoms
    left16 = iota((16, LANES), 1) < atoms
    left64 = lane64 < atoms
    other = jnp.bitwise_and(lane64, atoms - 1)
    latest = jnp.maximum(sub64, other).astype(F32)
    distinct = sub64 != other
    keep_left = jnp.where(left64, 1.0, 0.0).astype(BF16)
    keep_right = jnp.where(left64, 0.0, 1.0).astype(BF16)
    per_group = LANES // head_width
    groups = heads // per_group
    half_scale = 0.5 / math.sqrt(head_width)
    decay_rows = [
        -jnp.where(left8[0:1], head_decay[:, 2 * t : 2 * t + 1], head_decay[:, 2 * t + 1 : 2 * t + 2])
        for t in range(heads // 2)
    ]
    empty = jnp.zeros((head_width, LANES), BF16)

    for copy in copies:
        copy.wait()
    for side, row in ((0, 0), (1, tiles + 1)):
        for c in range(8):
            ext[c, row : row + 1, :] = rim_in[0, side, c : c + 1, :]
    ext[7] = TIME_STEP / ext[7]
    shared = (iota((2, LANES), 0) == 0) == (iota((2, LANES), 1) >= HALO)

    def gather(components):
        field = jnp.concatenate([ext[c] for c in components], axis=1)
        high = field.astype(BF16)
        rest = field - high.astype(F32)
        middle = rest.astype(BF16)
        low = (rest - middle.astype(F32)).astype(BF16)
        picked = dot_nn(pick, jnp.concatenate([high, middle, low], axis=0))
        result = []
        for c in range(len(components)):
            span = slice(c * LANES, (c + 1) * LANES)
            result.append(
                jnp.where(
                    pick_first,
                    lane_pick(picked[0:slots, span], pick_lane),
                    lane_pick(picked[slots:, span], pick_lane),
                )
            )
        return result

    quads = pairs // 2
    many = range(pairs)
    nothing = jnp.zeros((48, LANES), BF16)

    norm_row = jnp.bitwise_and(sub8, 3) == 0
    own_lanes = (sub8 < 4) == left8

    def set_places(centred):
        norm = centred[0] * centred[0] + centred[1] * centred[1] + centred[2] * centred[2]
        for c, values in enumerate([norm] + centred):
            places[:, c, :] = values[0:pairs]
            places[:, c + 4, :] = values[pairs:]

    def distance_factors(pair):
        place = places[pair]
        high = place.astype(BF16).astype(F32)
        middle = (place - high).astype(BF16).astype(F32)
        low = place - high - middle
        high_one = jnp.where(norm_row, 1.0, high)
        left = [high, middle, low, high_one, jnp.where(norm_row, 1.0, middle), high_one]
        once = jnp.where(norm_row, 1.0, -2.0 * high)
        cross = -2.0 * middle
        right = [
            once,
            once,
            once,
            jnp.where(norm_row, high, cross),
            jnp.where(norm_row, middle, cross),
            jnp.where(norm_row, low, -2.0 * low),
        ]
        right = [jnp.where(own_lanes, part, 0.0) for part in right]
        return jnp.concatenate(left, axis=0), jnp.concatenate(right, axis=0).astype(BF16)

    def model():
        far, hidden = [], []
        for u in range(quads):
            left, right = zip(distance_factors(2 * u), distance_factors(2 * u + 1))
            left = jnp.transpose(jnp.concatenate(left, axis=0))[0:atoms].astype(BF16)
            right = jnp.concatenate(
                [
                    jnp.concatenate([right[0], nothing], axis=0),
                    jnp.concatenate([nothing, right[1]], axis=0),
                ],
                axis=1,
            )
            squared = dot_nn(left, right)
            for v in range(2):
                inside = latest < counts[2 * u + v : 2 * u + v + 1, :]
                apart = jnp.maximum(squared[:, v * LANES : (v + 1) * LANES], 0.0)
                far.append(jnp.where(inside, jnp.where(distinct, apart, 0.0), FAR))
        summed = []
        for k in many:
            nearby = jnp.where(distinct, jnp.exp(-NEAR_RATE * far[k]), 0.0)
            near_hi = nearby.astype(BF16)
            near_lo = (nearby - near_hi.astype(F32)).astype(BF16)
            block = jnp.concatenate(
                [
                    jnp.concatenate([near * keep_left, near * keep_right], axis=0)
                    for near in (near_hi, near_lo)
                ],
                axis=1,
            )
            span = slice(k * LANES, (k + 1) * LANES)
            theirs = neigh_rows[span, :]
            summed.append(dot_nn(block, jnp.concatenate([theirs, theirs], axis=0)))
        for k in many:
            span = slice(k * LANES, (k + 1) * LANES)
            hidden.append(silu_of_double(summed[k] + own_rows[span, :]).astype(BF16))
        query, key, value, base, reads = {}, {}, {}, {}, {}
        parts, weights, mixed, lefts = {}, {}, {}, {}

        def project(u):
            block = jnp.concatenate(hidden[2 * u : 2 * u + 2], axis=0)
            query[u] = dot_nn(block, w_query[...]).astype(BF16)
            across = dot_nt(projections[...], block)
            key[u] = across[0:width].astype(BF16)
            value[u] = across[width : 2 * width].astype(BF16)
            base[u] = across[2 * width : 2 * width + 16] + across[2 * width + 16 :]

        def read(u):
            product = dot_nn(head_readout[...], value[u])
            reads[u] = product[0 : 16 * heads] + product[16 * heads :]

        def score(k):
            u, span = k // 2, slice((k % 2) * LANES, (k % 2 + 1) * LANES)
            straight = key[u][:, span]
            turned = pltpu.roll(straight, atoms, 1)
            result = []
            for m in range(2):
                at = (2 * (k % 2) + m) * atoms
                scored = []
                for g in range(groups):
                    blocks = []
                    for h in range(per_group):
                        feature = slice(
                            g * LANES + h * head_width, g * LANES + (h + 1) * head_width
                        )
                        source = straight if h % 2 == m else turned
                        keep = keep_left if h % 2 == 0 else keep_right
                        piece = source[feature] * keep[0:head_width]
                        blocks.append(
                            jnp.concatenate(
                                [piece if t == h // 2 else empty for t in range(per_group // 2)],
                                axis=1,
                            )
                        )
                    scored.append(
                        dot_nn(
                            query[u][at : at + atoms, g * LANES : (g + 1) * LANES],
                            jnp.concatenate(blocks, axis=0),
                        )
                    )
                result.append(scored)
            parts[k] = result

        def weigh(k):
            turned = pltpu.roll(far[k], atoms, 1)
            result = []
            for m in range(2):
                here = jnp.where(left64, far[k], turned) if m == 0 else jnp.where(left64, turned, far[k])
                tiles_out = []
                for t in range(heads // 2):
                    part = parts[k][m][t // 2][:, (t % 2) * LANES : (t % 2 + 1) * LANES]
                    envelope = jnp.exp(here * decay_rows[t])
                    tiles_out.append((silu_of_double(part * half_scale) * envelope).astype(BF16))
                result.append(jnp.concatenate(tiles_out, axis=1))
            weights[k] = jnp.concatenate(result, axis=0)

        def mix(k):
            u, span = k // 2, slice((k % 2) * LANES, (k % 2 + 1) * LANES)
            straight = reads[u][:, span]
            turned = pltpu.roll(straight, atoms, 1)
            left = []
            for m in range(2):
                a, b = (straight, turned) if m == 0 else (turned, straight)
                left.append(
                    jnp.concatenate(
                        [
                            jnp.where(
                                left16,
                                a[32 * t : 32 * t + 16],
                                b[32 * t + 16 : 32 * t + 32],
                            )
                            for t in range(heads // 2)
                        ],
                        axis=1,
                    )
                )
            left = jnp.concatenate(left, axis=0)
            left_hi = left.astype(BF16)
            left_lo = (left - left_hi.astype(F32)).astype(BF16)
            product = dot_nt(jnp.concatenate([left_hi, left_lo], axis=0), weights[k])
            mixed[k] = product[0:32] + product[32:64]

        def flatten(k):
            u, span = k // 2, slice((k % 2) * LANES, (k % 2 + 1) * LANES)
            scalars = jnp.where(left16, mixed[k][0:16], mixed[k][16:32]) + base[u][:, span]
            atom_energy[k : k + 1, :] = scalars[heads : heads + 1]
            straight = scalars[0:heads]
            turned = pltpu.roll(straight, atoms, 1)
            place = places[k]
            swapped = pltpu.roll(place, 4, 0)
            left = []
            for m in range(2):
                low, high = (straight, turned) if m == 0 else (turned, straight)
                a, b = (place, swapped) if m == 0 else (swapped, place)
                spot = jnp.where(norm_row, 1.0, jnp.where(sub8 < 4, a, b))
                terms = []
                for t in range(heads // 2):
                    flat = jnp.where(left8, low[2 * t : 2 * t + 1], high[2 * t + 1 : 2 * t + 2])
                    term = flat * spot
                    term_hi = term.astype(BF16).astype(F32)
                    terms.append(jnp.where(sub8 < 4, term_hi, term - term_hi))
                left.append(jnp.concatenate(terms, axis=1))
            lefts[k] = jnp.concatenate(left, axis=0).astype(BF16)

        def pull(k):
            pulled = dot_nt(lefts[k], weights[k])
            pulls[k] = jnp.where(left8, pulled[0:8], pulled[8:16])

        steps = dict(
            project=project, read=read, score=score, weigh=weigh, mix=mix, flatten=flatten, pull=pull
        )
        for name, k in order_of_work(quads):
            steps[name](k)

    def finish_energy(step):
        each = atom_energy[...]
        energy = jnp.concatenate(
            [
                jnp.sum(jnp.where(left_rows, each, 0.0), axis=1, keepdims=True),
                jnp.sum(jnp.where(left_rows, 0.0, each), axis=1, keepdims=True),
            ],
            axis=0,
        )
        energies_out[step : step + 1, :] = to_row(energy)

    def hand_out(which):
        for tile in which:
            span = pl.ds(tile * LANES, LANES)
            for c in range(3):
                positions_out[c : c + 1, span] = ext[c, tile + 1 : tile + 2, :]
                velocities_out[c : c + 1, span] = ext[4 + c, tile + 1 : tile + 2, :]

    for step in range(STEPS):
        fields = gather((0, 1, 2, 3) if step == 0 else (0, 1, 2))
        centred = [field - field[:, 0:1] for field in fields[:3]]
        for c in range(3):
            rows[c] = jnp.where(left_rows, centred[c][0:pairs], centred[c][pairs:])
        set_places(centred)
        if step == 0:
            sort = jnp.where(half_lane.astype(F32) < count, fields[3], -1.0)
            cols[...] = jnp.transpose(jnp.concatenate([sort] * (LANES // slots), axis=0))[0:atoms]
            both_tables = jnp.concatenate([embed[...] * 0.5, neigh[...] * 0.5], axis=1).astype(BF16)

            for u in range(quads):
                hot = []
                for k in (2 * u, 2 * u + 1):
                    for m in range(2):
                        at = jnp.full((atoms, LANES), m * pairs + k, jnp.int32)
                        kind = lane_pick(cols[...], at)
                        hot.append(jnp.where(kind == lane64.astype(F32), 1.0, 0.0))
                hot = jnp.concatenate(hot, axis=0).astype(BF16)[:, 0:types]
                found = dot_nn(hot, both_tables)
                span = slice(2 * u * LANES, (2 * u + 2) * LANES)
                own_rows[span, :] = found[:, 0:width]
                neigh_rows[span, :] = found[:, width:].astype(BF16)
        model()

        sums = [pulls[:, q, :] + pulls[:, q + 4, :] for q in range(4)]
        placed_here, placed_next = [], []
        for c in range(3):
            force = rows[c] * sums[0] - sums[c + 1]
            force = jnp.concatenate(
                [jnp.where(left_rows, force, 0.0), jnp.where(left_rows, 0.0, force)], axis=0
            )
            turned = lane_pick(force, put_lane)
            placed_here.append(jnp.where(put_first, turned, 0.0))
            placed_next.append(jnp.where(put_first, 0.0, turned))
        placed = jnp.concatenate(
            [jnp.concatenate(placed_here, axis=1), jnp.concatenate(placed_next, axis=1)], axis=0
        )
        placed_hi = placed.astype(BF16)
        placed_lo = (placed - placed_hi.astype(F32)).astype(BF16)
        total = dot_nn(put, jnp.concatenate([placed_hi, placed_lo], axis=0))
        total = [total[:, c * LANES : (c + 1) * LANES] for c in range(3)]

        phase = step + 1
        for c in range(3):
            rim_out[phase, 0, 2 * c : 2 * c + 2, :] = total[c][tiles : tiles + 2]
            rim_out[phase, 1, 2 * c : 2 * c + 2, :] = total[c][0:2]
        copies = exchange(phase)
        for c in range(3):
            moved = ext[4 + c] + total[c] * ext[7]
            ext[4 + c] = moved
            ext[c] = ext[c] + TIME_STEP * moved
        finish_energy(step)
        if step == STEPS - 1:
            hand_out(range(1, tiles - 1))
        for copy in copies:
            copy.wait()
        for side, row in ((0, 0), (1, tiles)):
            border = slice(row, row + 2)
            for c in range(3):
                extra = jnp.where(shared, rim_in[phase, side, 2 * c : 2 * c + 2, :], 0.0)
                kick = extra * ext[7, border, :]
                ext[4 + c, border, :] = ext[4 + c, border, :] + kick
                ext[c, border, :] = ext[c, border, :] + TIME_STEP * kick
    hand_out((0, tiles - 1))


def hand_over(*refs):
    for k in range(3):
        refs[k + 3][...] = refs[k][...]


def body(
    positions,
    velocities,
    masses,
    atom_kinds,
    frag_atoms,
    assign,
    embed_table,
    neigh_table,
    w_query,
    w_key,
    w_value,
    w_energy,
    w_force,
    head_decay,
):
    tiles = positions.shape[1] // LANES
    slots, atoms = frag_atoms.shape
    heads = head_decay.shape[0]
    width = w_query.shape[0]
    ext_rows = -(-(tiles + 3) // 8) * 8
    vmem = pl.BlockSpec(memory_space=pltpu.VMEM)
    operands = (
        positions,
        velocities,
        masses.reshape(tiles, LANES),
        atom_kinds.reshape(tiles, LANES),
        frag_atoms,
        assign,
        embed_table,
        neigh_table,
        w_query,
        w_key,
        w_value,
        w_energy.reshape(1, width),
        w_force.T,
        head_decay.reshape(1, heads),
    )
    results = pl.pallas_call(
        functools.partial(kernel, tiles, slots, heads),
        out_shape=(
            jax.ShapeDtypeStruct(positions.shape, F32),
            jax.ShapeDtypeStruct(velocities.shape, F32),
            jax.ShapeDtypeStruct((STEPS, slots), F32),
        ),
        in_specs=[pl.BlockSpec(memory_space=pltpu.HBM)] * OPERANDS,
        out_specs=(vmem, vmem, vmem),
        scratch_shapes=[pltpu.VMEM(operand.shape, operand.dtype) for operand in operands]
        + [
            pltpu.VMEM((8, ext_rows, LANES), F32),
            pltpu.VMEM((STEPS + 1, 2, 8, LANES), F32),
            pltpu.VMEM((STEPS + 1, 2, 8, LANES), F32),
            pltpu.VMEM((3, slots // 2, LANES), F32),
            pltpu.VMEM((atoms, LANES), F32),
            pltpu.VMEM((slots // 2, LANES), F32),
            pltpu.VMEM((slots // 2, 8, LANES), F32),
            pltpu.VMEM((slots * atoms, width), F32),
            pltpu.VMEM((slots * atoms, width), BF16),
            pltpu.VMEM((2 * width + 32, width), BF16),
            pltpu.VMEM((32 * heads, width), BF16),
            pltpu.VMEM((slots // 2, 8, LANES), F32),
            pltpu.VMEM((slots // 2, LANES), F32),
            pltpu.SemaphoreType.DMA((OPERANDS,)),
            pltpu.SemaphoreType.DMA((STEPS + 1, 2)),
            pltpu.SemaphoreType.DMA((STEPS + 1, 2)),
        ],
        compiler_params=pltpu.CompilerParams(
            collective_id=0, has_side_effects=True, vmem_limit_bytes=56 * 1024 * 1024
        ),
    )(*operands)
    return pl.pallas_call(
        hand_over,
        out_shape=tuple(jax.ShapeDtypeStruct(result.shape, F32) for result in results),
        in_specs=[vmem] * 3,
        out_specs=(vmem,) * 3,
        compiler_params=pltpu.CompilerParams(vmem_limit_bytes=56 * 1024 * 1024),
    )(*results)


def solution(mesh):
    both = ("dom", "grp")
    return jax.shard_map(
        body,
        mesh=mesh,
        in_specs=(
            P(None, both),
            P(None, both),
            P(both),
            P(both),
            P(both, None),
            P(None, both),
        )
        + (P(),) * 8,
        out_specs=(P(None, both), P(None, both), P(None, both)),
        check_vma=False,
    )
```
